256 devices in a mesh: blk: 8 (over x, y_hi), ep: 32 (over z, y_lo, core).
Axes of the slice: x: 4, y: 4 (y_hi: 2, y_lo: 2; y = y_hi * 2 + y_lo), z: 8, core: 2. Of those that a mesh axis runs over, the one named last changes fastest.
Arguments:
- queries: bfloat16 [1024, 32, 6144], P('blk', 'ep'), may hold values from -4.6 to 4.6
- keys: bfloat16 [1024, 32, 1024], P('blk', 'ep'), may hold values from -4.6 to 4.6
- values: bfloat16 [1024, 32, 1024], P('blk', 'ep'), may hold values from -4 to 4
- doc_lengths: int32 [32, 8], P('ep'), may hold values from 1 to 512, 1024 in all within a row
- hidden: bfloat16 [1024, 32, 5120], P('blk', 'ep'), may hold values from -36 to 36
- norm_gain: bfloat16 [5120], replicated, may hold values from 0.099609375 to 1.8984375
- token_ids: int32 [1024, 32], P('blk', 'ep'), may hold values from 0 to 151551
- expert_table: int32 [151552], replicated, may hold values from 0 to 31
- w_gate: bfloat16 [32, 1536, 5120], P('ep', 'blk'), may hold values from -0.078125 to 0.078125
- w_up: bfloat16 [32, 1536, 5120], P('ep', 'blk'), may hold values from -0.078125 to 0.078125
- w_down: bfloat16 [32, 1536, 5120], P('ep', 'blk'), may hold values from -0.15625 to 0.15625
Outputs:
- attn_out: bfloat16 [1024, 32, 6144], P('blk', 'ep')
- moe_out: bfloat16 [1024, 32, 5120], P('blk', 'ep')
The draws below stay inside these ranges and needn't reach their ends.
All inputs are finite; a program needn't handle non-finite values.
Results may differ from the reference program's by a relative error of at most 0.012.
Values may be sent and summed in bfloat16 or wider, within the bound.
A program may use at most 128 MiB of HBM per device.

```python
import math
import jax
import jax.numpy as jnp
import numpy as np
from jax import lax

D = 5120
HQ = 48
HK = 8
HD = 128
FF = 1536
VOCAB = 151552
DOCS = 8
TOK_DEV = 128
EXPERTS = 32
LEN = 1024
SEQS = 32
DOC_MOST = 512
CAP = 4
N_BLK = 8


def draw_queries(key, part):
    base_key = jax.random.fold_in(key, 1)
    groups = HQ // HK
    base = jax.random.truncated_normal(base_key, -4.0, 4.0, (LEN, SEQS, HK, groups, HD), jnp.float32)
    return base.reshape(LEN, SEQS, HQ * HD).astype(jnp.bfloat16)


def draw_keys(key, part):
    base_key = jax.random.fold_in(key, 2)
    base = jax.random.truncated_normal(base_key, -4.0, 4.0, (LEN, SEQS, HK, HD), jnp.float32)
    return base.reshape(LEN, SEQS, HK * HD).astype(jnp.bfloat16)


def draw_hidden(key, part):
    key = jax.random.fold_in(key, 3)
    row_scale = jnp.exp(jax.random.uniform(jax.random.fold_in(key, 11), (LEN, SEQS, 1), jnp.float32, jnp.log(0.3), jnp.log(3.0)))
    col_scale = jnp.exp(jax.random.uniform(jax.random.fold_in(key, 12), (D,), jnp.float32, jnp.log(0.3), jnp.log(3.0)))
    noise = jax.random.truncated_normal(jax.random.fold_in(key, 13), -4.0, 4.0, (LEN, SEQS, D), jnp.float32)
    return (noise * row_scale * col_scale).astype(jnp.bfloat16)


def touch_ends(drawn, stream_key, low, high):
    extent = drawn.shape
    index_at = [jax.random.randint(jax.random.fold_in(stream_key, axis), (), 0, extent[axis]) for axis in range(len(extent))]
    drawn = drawn.at[tuple(index_at)].set(low)
    longest = extent.index(max(extent))
    index_at[longest] = (index_at[longest] + 1) % extent[longest]
    return drawn.at[tuple(index_at)].set(high)


def level_of(key, dims, cuts, low, largest):
    gain, own = 1.0, jax.random.fold_in(key, 6)
    for dim, blocks in cuts:
        heights = jnp.exp(jax.random.uniform(jax.random.fold_in(own, dim), (blocks,), jnp.float32, low / len(cuts), largest / len(cuts)))
        gain = gain * jnp.repeat(heights, dims[dim] // blocks).reshape([-1 if axis == dim else 1 for axis in range(len(dims))])
    return gain


def wide_ids(rng, dims, number_of, slope):
    weights = [min(1 << octave, number_of + 1 - (1 << octave)) * (1 << 20) // math.isqrt((1 << octave) ** slope) + 1 for octave in range((number_of + 1).bit_length()) if 1 << octave <= number_of]
    spread = 1 + sum(weights) // (1 << 30)
    table = np.cumsum(np.array([max(1, weight // spread) for weight in weights]))
    pick = jax.random.randint(jax.random.fold_in(rng, 1), dims, 0, int(table[len(weights) - 1]))
    start = jnp.left_shift(1, jnp.searchsorted(jnp.asarray(table, jnp.int32), pick, side="right").astype(jnp.int32))
    standing = start - 1 + jax.random.randint(jax.random.fold_in(rng, 4), dims, 0, 1 << 30) % jnp.minimum(start, number_of + 1 - start)
    return jax.random.permutation(jax.random.fold_in(rng, 2), number_of)[standing].astype(jnp.int32)


def profile(count, total, limit, lean):
    weights = [(1 << 20) // math.isqrt(standing ** lean) + 1 for standing in range(2, count + 1)]
    surplus, given = total - limit - (count - 1), [1] * (count - 1)
    while surplus > 0:
        movable = [i for i in range(count - 1) if given[i] < limit]
        pool, left = sum([weights[i] for i in movable]), surplus
        for i in movable:
            more = min(limit - given[i], max(1, left * weights[i] // pool), surplus)
            given[i] = given[i] + more
            surplus = surplus - more
    return np.array([limit] + given)


def ragged(stream_key, number_of, total, reach, slope):
    if number_of == 2:
        one = jax.random.randint(stream_key, (), max(1, total - reach), min(reach, total - 1) + 1)
        return jnp.stack([one, total - one])
    tallies = jnp.asarray(profile(number_of, total, reach, slope), jnp.int32)
    twos = (number_of - 1) // 2
    giver, taker = tallies[1:1 + 2 * twos:2], tallies[2:2 + 2 * twos:2]
    room = jnp.minimum(giver - 1, reach - taker)
    moved = jax.random.randint(jax.random.fold_in(stream_key, 1), (twos,), 0, 1 << 20) % (room + 1)
    tallies = tallies.at[1:1 + 2 * twos:2].set(giver - moved).at[2:2 + 2 * twos:2].set(taker + moved)
    return tallies[jax.random.permutation(jax.random.fold_in(stream_key, 2), number_of)]


def normal_values(key, shape, width, most, cuts=(), kind=jnp.bfloat16):
    entries = jax.random.normal(key, shape, jnp.float32) * width
    if len(cuts) > 0:
        entries = level_of(key, shape, cuts, -0.22, 0.18) * entries
    return jnp.clip(entries, min=-most, max=most).astype(kind)


def setup_inputs(seed: int = 0) -> dict:
    streams_of = jax.random.split(jax.random.key(seed), 12)
    queries = draw_queries(jax.random.fold_in(streams_of[11], 71), 0)
    keys = draw_keys(jax.random.fold_in(streams_of[11], 71), 0)
    values = normal_values(streams_of[2], (LEN, SEQS, HK * HD), 1.0, 4.0, ((0, 8), (1, 32)))
    doc_lengths = jax.vmap(lambda own: ragged(own, DOCS, LEN, DOC_MOST, 2))(jax.random.split(streams_of[3], SEQS)).reshape((SEQS, DOCS)).astype(jnp.int32)
    hidden = draw_hidden(jax.random.fold_in(streams_of[11], 71), 0)
    norm_gain = jnp.clip(1.0 + 0.18 * jax.random.normal(streams_of[5], (D,), jnp.float32), 0.099609375, 1.8984375).astype(jnp.bfloat16)
    token_ids = touch_ends(wide_ids(streams_of[6], (LEN, SEQS), VOCAB, 2), jax.random.fold_in(streams_of[6], 3), 0, VOCAB - 1).astype(jnp.int32)
    expert_table = touch_ends(jax.random.randint(streams_of[7], (VOCAB,), 0, EXPERTS), jax.random.fold_in(streams_of[7], 1), 0, EXPERTS - 1).astype(jnp.int32)
    w_gate = normal_values(streams_of[8], (EXPERTS, FF, D), D ** -0.5, 0.078125, ((0, 32), (1, 8)))
    w_up = normal_values(streams_of[9], (EXPERTS, FF, D), D ** -0.5, 0.078125, ((0, 32), (1, 8)))
    w_down = normal_values(streams_of[10], (EXPERTS, FF, D), FF ** -0.5, 0.15625, ((0, 32), (1, 8)))
    return {"queries": queries, "keys": keys, "values": values, "doc_lengths": doc_lengths, "hidden": hidden, "norm_gain": norm_gain, "token_ids": token_ids, "expert_table": expert_table, "w_gate": w_gate, "w_up": w_up, "w_down": w_down}


def segment_table(doc_lengths):
    doc_ends = jnp.cumsum(doc_lengths, axis=-1).astype(jnp.int32)
    places = jnp.arange(LEN, dtype=jnp.int32)
    hits = (places[None, :, None] >= doc_ends[:, None, :]).astype(jnp.int32)
    return lax.optimization_barrier(jnp.sum(hits, axis=-1)).astype(jnp.int32)

def attend_sequence(operands):
    query_rows, key_rows, value_rows, segment = operands
    groups = HQ // HK
    query_wide = query_rows.reshape(LEN, HK, groups, HD).astype(jnp.float32)
    key_wide = key_rows.reshape(LEN, HK, HD).astype(jnp.float32)
    value_wide = value_rows.reshape(LEN, HK, HD).astype(jnp.float32)
    scores = jnp.einsum('qhgd,khd->hgqk', query_wide, key_wide) / math.sqrt(HD)
    places = jnp.arange(LEN, dtype=jnp.int32)
    allowed = (places[None, :] <= places[:, None]) & (segment[None, :] == segment[:, None])
    masked = jnp.where(allowed, scores, jnp.float32(-1e+30))
    top_score = lax.optimization_barrier(jnp.max(masked, axis=-1, keepdims=True))
    weight = jnp.where(allowed, jnp.exp(masked - top_score), jnp.float32(0.0))
    total = lax.optimization_barrier(jnp.sum(weight, axis=-1))
    rounded = lax.optimization_barrier(weight.astype(jnp.bfloat16)).astype(jnp.float32)
    mixed = jnp.einsum('hgqk,khd->qhgd', rounded, value_wide)
    mixed = mixed / jnp.transpose(total, (2, 0, 1))[..., None]
    return mixed.reshape(LEN, HQ * HD).astype(jnp.bfloat16)

def expert_block(operands):
    rows, gate_rows, up_rows, down_rows = operands
    gate = jnp.dot(rows, gate_rows.T, preferred_element_type=jnp.float32)
    up_proj = jnp.dot(rows, up_rows.T, preferred_element_type=jnp.float32)
    act = lax.optimization_barrier((jax.nn.silu(gate) * up_proj).astype(jnp.bfloat16))
    row_count = rows.shape[0]
    act_wide = act.astype(jnp.float32).reshape(row_count, N_BLK, FF // N_BLK)
    down_wide = down_rows.astype(jnp.float32).reshape(N_BLK, FF // N_BLK, D)
    parts = jnp.einsum('rjf,jfd->jrd', act_wide, down_wide)
    parts = lax.optimization_barrier(parts.astype(jnp.bfloat16)).astype(jnp.float32)
    return lax.optimization_barrier(jnp.sum(parts, axis=0)).astype(jnp.bfloat16)

def reference(queries, keys, values, doc_lengths, hidden, norm_gain, token_ids, expert_table, w_gate, w_up, w_down):
    segment = segment_table(doc_lengths)
    attended = lax.map(attend_sequence, (jnp.transpose(queries, (1, 0, 2)), jnp.transpose(keys, (1, 0, 2)), jnp.transpose(values, (1, 0, 2)), segment))
    attn_out = jnp.transpose(attended, (1, 0, 2))
    wide = hidden.astype(jnp.float32)
    normed = (wide * lax.rsqrt(lax.optimization_barrier(jnp.mean(wide * wide, axis=-1, keepdims=True)) + 1e-05) * norm_gain.astype(jnp.float32)).astype(jnp.bfloat16)
    expert = expert_table[token_ids].astype(jnp.int32)
    blocked = expert.reshape(N_BLK, TOK_DEV, SEQS)
    onehot = (blocked[..., None] == jnp.arange(EXPERTS, dtype=jnp.int32)).astype(jnp.int32)
    before = jnp.cumsum(onehot, axis=1) - onehot
    rank = lax.optimization_barrier(jnp.sum(before * onehot, axis=-1)).astype(jnp.int32)
    kept = rank < CAP
    rows_each = N_BLK * SEQS * CAP
    block_index = jnp.arange(N_BLK, dtype=jnp.int32)[:, None, None]
    seq_index = jnp.arange(SEQS, dtype=jnp.int32)[None, None, :]
    slot = (block_index * SEQS + seq_index) * CAP + rank + blocked * rows_each
    target = jnp.where(kept, slot, EXPERTS * rows_each).astype(jnp.int32).reshape(-1)
    buffer = jnp.zeros((EXPERTS * rows_each, D), jnp.bfloat16)
    buffer = buffer.at[target].set(normed.reshape(-1, D), mode='drop')
    results = lax.map(expert_block, (buffer.reshape(EXPERTS, rows_each, D), w_gate, w_up, w_down))
    flat = results.reshape(-1, D)
    picked = flat[jnp.minimum(target, EXPERTS * rows_each - 1).astype(jnp.int32)]
    moe_out = jnp.where(kept.reshape(-1)[:, None], picked, jnp.zeros_like(picked)).reshape(LEN, SEQS, D)
    return (attn_out, moe_out)
```

```python
import functools
import math

import jax
import jax.numpy as jnp
from jax import lax
from jax.experimental import pallas as pl
from jax.experimental.pallas import tpu as pltpu
from jax.sharding import PartitionSpec as P

HQ = 48
HK = 8
HD = 128
GROUPS = HQ // HK
D = 5120
FB = 192
TOK = 128
CAP = 4
NX, NH, NZ = 4, 2, 8
NEP = 32
VROWS = 1184
QW = D // 4

NC = 4
SEND = NEP // NC
R = SEND * CAP
M = SEND * 16
W1 = 3328
W2 = D - W1
H1, H2 = W1 // 2, W2 // 2
HALF = D // 2
WIN = 5 * TOK
BLOCK_BACK = (0, 2, 4, 1, 3)

F32 = jnp.float32
BF16 = jnp.bfloat16
MESH = pl.DeviceIdType.MESH


def z_step(pos):
    return (pos + 1) // 2 if pos % 2 else (NZ - pos // 2) % NZ


def iota(shape, dim):
    return lax.broadcasted_iota(jnp.int32, shape, dim)


def layer_kernel(
    doc_ref, tok_ref, table_ref, gain_ref, hid_ref, q_hbm, k_hbm, v_hbm, wg_hbm, wu_hbm, wd_hbm,
    attn_ref, moe_ref,
    q_ref, kv, bias, wgu, wd, normed, spread, out_msg, in_msg, ret_out, ret_in,
    xs, ps, r_y, r_h1, r_m1, r_t, r_h2, r_m2, fin,
    s_loc, s_kv, r_kv, s_a2a, r_a2a, s_ret, r_ret, s_ag, r_ag, s_rs, r_rs,
):
    b = lax.axis_index("blk")
    e = lax.axis_index("ep")
    x, h = b // 2, b % 2
    z, yl, core = e // 4, (e // 2) % 2, e % 2

    def at_x(step):
        return (((x + step) % NX) * 2 + h, e)

    at_y = (x * 2 + (h + 1) % 2, e)

    def at_ep(k, sign):
        dz, fy, dc = z_step(k // 4), (k // 2) % 2, k % 2
        zz = (z + (dz if sign > 0 else NZ - dz)) % NZ
        return (b, (zz * 2 + (yl + fy) % 2) * 2 + (core + dc) % 2)

    barrier = pltpu.get_barrier_semaphore()
    peers = [at_x(1), at_x(2), at_x(3), at_y] + [at_ep(k, 1) for k in range(1, NEP)]
    for peer in peers:
        pl.semaphore_signal(barrier, inc=1, device_id=peer, device_id_type=MESH)

    local = []
    for i, (src, dst) in enumerate(
        (
            (k_hbm, kv.at[0, 0]),
            (v_hbm, kv.at[0, 1]),
            (q_hbm, q_ref),
            (wg_hbm, wgu.at[0:FB]),
            (wu_hbm, wgu.at[FB : 2 * FB]),
            (wd_hbm, wd),
        )
    ):
        cp = pltpu.make_async_copy(src, dst, s_loc.at[i])
        cp.start()
        local.append(cp)

    pl.semaphore_wait(barrier, len(peers))

    sent = []

    def push(src, dst, send_sem, recv_sem, device):
        cp = pltpu.make_async_remote_copy(
            src_ref=src, dst_ref=dst, send_sem=send_sem, recv_sem=recv_sem,
            device_id=device, device_id_type=MESH,
        )
        cp.start()
        sent.append(cp)
        return cp

    kv_in = [
        push(src, kv.at[step, i], s_kv.at[step * 2 - 2 + i], r_kv.at[step * 2 - 2 + i], at_x(step))
        for step in (1, 2)
        for i, src in ((0, k_hbm), (1, v_hbm))
    ]

    def norm_rows(i, carry):
        rows = pl.ds(pl.multiple_of(i * 16, 16), 16)
        wide = hid_ref[rows, :].astype(F32)
        scale = lax.rsqrt(jnp.sum(wide * wide, axis=1, keepdims=True) * (1.0 / D) + 1e-05)
        normed[rows, :] = (wide * scale * gain_ref[...]).astype(BF16)
        return carry

    lax.fori_loop(0, TOK // 16, norm_rows, 0)

    eye = iota((TOK, TOK), 0) == iota((TOK, TOK), 1)
    lane = iota((TOK, TOK), 1)
    tok = tok_ref[...]
    tok_hi, tok_lo = (tok // 128).astype(F32), (tok % 128).astype(F32)
    hi_col = jnp.sum(jnp.where(eye, tok_hi, 0.0), axis=1, keepdims=True)
    lo_col = jnp.sum(jnp.where(eye, tok_lo, 0.0), axis=1, keepdims=True)
    pick = (iota((TOK, VROWS), 1).astype(F32) == hi_col).astype(F32).astype(BF16)
    row = jnp.dot(pick, table_ref[...].astype(F32).astype(BF16), preferred_element_type=F32)
    expert = jnp.sum(jnp.where(lane.astype(F32) == lo_col, row, 0.0), axis=1, keepdims=True)
    onehot = (lane.astype(F32) == expert).astype(F32)
    earlier = (lane < iota((TOK, TOK), 0)).astype(F32).astype(BF16)
    before = jnp.dot(earlier, onehot.astype(BF16), preferred_element_type=F32)
    rank = jnp.sum(before * onehot, axis=1, keepdims=True)
    slot_col = jnp.where(rank < CAP, expert * CAP + rank, -1.0)
    slot_row = jnp.sum(jnp.where(eye, slot_col, 0.0), axis=0, keepdims=True)

    def slot_of(i):
        k = i // 16
        pos = k // 4
        dz = jnp.where(pos % 2 == 1, (pos + 1) // 2, (NZ - pos // 2) % NZ)
        other = (((z + dz) % NZ) * 2 + (yl + (k // 2) % 2) % 2) * 2 + (core + k % 2) % 2
        return other * CAP + i % 4, (i // 4) % 4

    msg_slot, msg_quarter = slot_of(iota((NEP * 16, TOK), 0))
    here = msg_slot.astype(F32) == slot_row
    for quarter in range(4):
        spread[quarter] = (here & (msg_quarter == quarter)).astype(F32).astype(BF16)

    for c in range(NC):
        rows = slice(c * M, (c + 1) * M)

        def spread_columns(n, carry):
            acc = jnp.zeros((M, 256), F32)
            for quarter in range(4):
                cols = pl.ds(pl.multiple_of(quarter * QW + n * 256, 128), 256)
                acc += jnp.dot(spread[quarter, rows, :], normed[:, cols], preferred_element_type=F32)
            out_msg[rows, pl.ds(pl.multiple_of(n * 256, 128), 256)] = acc.astype(BF16)
            return carry

        lax.fori_loop(0, QW // 256, spread_columns, 0)
        for k in range(max(1, c * SEND), (c + 1) * SEND):
            at = slice(k * 16, (k + 1) * 16)
            pltpu.make_async_remote_copy(
                src_ref=out_msg.at[at], dst_ref=in_msg.at[at], send_sem=s_a2a.at[c],
                recv_sem=r_a2a.at[c], device_id=at_ep(k, 1), device_id_type=MESH,
            ).start()
    in_msg[0:16, :] = out_msg[0:16, :]

    def wait_messages(ref, sem, c):
        part = ref.at[max(16, c * M) : (c + 1) * M]
        pltpu.make_async_copy(part, part, sem.at[c]).wait()

    last = 0
    ends = []
    for i in range(8):
        last = last + doc_ref[0, i]
        ends.append(last)
    q_pos = b * TOK + iota((TOK, TOK), 0)
    start = jnp.zeros((TOK, TOK), jnp.int32)
    for end in ends:
        start = jnp.where(q_pos >= end, end, start)
    for s, back in enumerate(BLOCK_BACK):
        k_pos = (b - back) * TOK + iota((TOK, TOK), 1)
        allowed = (k_pos >= start) & (k_pos <= q_pos)
        bias[:, s * TOK : (s + 1) * TOK] = jnp.where(allowed, 0.0, -1e30).astype(F32)

    kv_fwd = []

    def forward_keys():
        for cp in kv_in:
            cp.wait_recv()
        local[0].wait()
        local[1].wait()
        for i in range(2):
            kv_fwd.append(push(kv.at[h + i], kv.at[3 + i], s_kv.at[4 + i], r_kv.at[4 + i], at_y))

    def attend_start():
        for cp in kv_fwd:
            cp.wait_recv()
        local[2].wait()

    def attend(first, count):
        def one(g, carry):
            head = pl.ds(pl.multiple_of(g * HD, HD), HD)
            wide = pl.ds(pl.multiple_of(g * GROUPS * HD, HD), GROUPS * HD)
            keys = kv[:, 0, :, head].reshape(WIN, HD)
            vals = kv[:, 1, :, head].reshape(WIN, HD)
            q_all = q_ref[:, wide]
            outs = []
            for i in range(GROUPS):
                q_one = q_all[:, i * HD : (i + 1) * HD]
                score = lax.dot_general(
                    q_one, keys, (((1,), (1,)), ((), ())), preferred_element_type=F32
                ) + bias[...]
                top = jnp.max(score, axis=1, keepdims=True)
                weight = jnp.exp((score - top) * (1.0 / math.sqrt(HD)))
                total = jnp.sum(weight, axis=1, keepdims=True)
                mixed = jnp.dot(weight.astype(BF16), vals, preferred_element_type=F32)
                outs.append((mixed / total).astype(BF16))
            attn_ref[:, wide] = jnp.concatenate(outs, axis=1)
            return carry

        lax.fori_loop(first, first + count, one, 0)

    def perm(shape, row_dim, quarter):
        rr, mm = iota(shape, row_dim), iota(shape, 1 - row_dim)
        same = (mm // 16 == rr // 4) & ((mm // 4) % 4 == quarter) & (mm % 4 == rr % 4)
        return same.astype(F32).astype(BF16)

    ag = [dict() for _ in range(NC)]
    rs = [dict() for _ in range(NC)]

    def ag_push(c, name, src, dst, device):
        i = len(ag[c])
        ag[c][name] = push(src, dst, s_ag.at[c, i], r_ag.at[c, i], device)

    def rs_push(c, name, src, dst, device):
        i = len(rs[c])
        rs[c][name] = push(src, dst, s_rs.at[c, i], r_rs.at[c, i], device)

    lo, hi = slice(0, HALF), slice(HALF, D)
    c1, c2 = slice(0, W1), slice(W1, D)
    c1a, c1b = slice(0, H1), slice(H1, W1)
    c2a, c2b = slice(W1, W1 + H2), slice(W1 + H2, D)

    def a0(c):
        wait_messages(in_msg, r_a2a, c)
        for quarter in range(4):
            xs[c, 0, :, quarter * QW : (quarter + 1) * QW] = jnp.dot(
                perm((R, M), 0, quarter), in_msg[c * M : (c + 1) * M, :], preferred_element_type=F32
            ).astype(BF16)
        own = xs.at[c, 0]
        ag_push(c, "1", own, xs.at[c, 1], at_x(1))
        ag_push(c, "3", own, xs.at[c, 3], at_x(3))
        ag_push(c, "4", own, xs.at[c, 4], at_y)

    def a1(c):
        def part(i, cols):
            return xs.at[c, i, :, cols]

        for name in "134":
            ag[c][name].wait_recv()
        ag_push(c, "2a", part(1, lo), part(2, lo), at_x(1))
        ag_push(c, "2b", part(3, hi), part(2, hi), at_x(3))
        ag_push(c, "5x", part(4, c1), part(5, c1), at_x(1))
        ag_push(c, "7x", part(4, c1), part(7, c1), at_x(3))
        ag_push(c, "5y", part(1, c2), part(5, c2), at_y)
        ag_push(c, "7y", part(3, c2), part(7, c2), at_y)

    def a2(c):
        def part(i, cols):
            return xs.at[c, i, :, cols]

        for name in ("2a", "2b", "5x", "7x"):
            ag[c][name].wait_recv()
        ag_push(c, "6a", part(5, c1a), part(6, c1a), at_x(1))
        ag_push(c, "6b", part(7, c1b), part(6, c1b), at_x(3))
        ag_push(c, "6y", part(2, c2), part(6, c2), at_y)

    def r0(c):
        for name in ("5y", "7y", "6a", "6b", "6y"):
            ag[c][name].wait_recv()
        rows = xs[c].reshape(8 * R, D)
        both = lax.dot_general(
            rows, wgu[...], (((1,), (1,)), ((), ())), preferred_element_type=F32
        )
        gate, up = both[:, :FB], both[:, FB:]
        act = (gate / (1.0 + jnp.exp(-gate)) * up).astype(BF16)

        def down(n, carry):
            cols = pl.ds(pl.multiple_of(n * 512, 128), 512)
            res = jnp.dot(act, wd[:, cols], preferred_element_type=F32).astype(BF16)
            ps[c, :, :, cols] = res.reshape(8, R, 512)
            return carry

        lax.fori_loop(0, D // 512, down, 0)
        rs_push(c, "h10a", ps.at[c, 2, :, c1a], r_h1.at[c, 0, 0], at_x(1))
        rs_push(c, "h10b", ps.at[c, 2, :, c1b], r_h1.at[c, 0, 1], at_x(3))
        rs_push(c, "y", ps.at[c, 4:8, :, c2], r_y.at[c], at_y)
        rs_push(c, "h11a", ps.at[c, 6, :, c1a], r_h1.at[c, 1, 0], at_x(1))
        rs_push(c, "h11b", ps.at[c, 6, :, c1b], r_h1.at[c, 1, 1], at_x(3))

    def add(c, i, cols, *terms):
        total = ps[c, i, :, cols].astype(F32)
        for term in terms:
            total = total + term.astype(F32)
        ps[c, i, :, cols] = total.astype(BF16)

    def r1(c):
        for name in ("h10a", "h10b", "h11a", "h11b"):
            rs[c][name].wait_recv()
        for dh in range(2):
            add(c, dh * 4 + 3, c1a, r_h1[c, dh, 0])
            add(c, dh * 4 + 1, c1b, r_h1[c, dh, 1])
            rs_push(c, "m1%d+" % dh, ps.at[c, dh * 4 + 3, :, c1], r_m1.at[c, dh, 0], at_x(1))
            rs_push(c, "m1%d-" % dh, ps.at[c, dh * 4 + 1, :, c1], r_m1.at[c, dh, 1], at_x(3))
        rs[c]["y"].wait_recv()
        add(c, 2, c2, r_y[c, 2])
        rs_push(c, "h2a", ps.at[c, 2, :, c2a], r_h2.at[c, 0], at_x(1))
        rs_push(c, "h2b", ps.at[c, 2, :, c2b], r_h2.at[c, 1], at_x(3))

    def r2(c):
        for name in ("m11+", "m11-"):
            rs[c][name].wait_recv()
        add(c, 4, c1, r_m1[c, 1, 0], r_m1[c, 1, 1])
        rs_push(c, "t", ps.at[c, 4, :, c1], r_t.at[c], at_y)
        for name in ("h2a", "h2b"):
            rs[c][name].wait_recv()
        add(c, 3, c2a, r_y[c, 3, :, 0:H2], r_h2[c, 0])
        add(c, 3, c2b, r_y[c, 3, :, H2:W2])
        add(c, 1, c2a, r_y[c, 1, :, 0:H2])
        add(c, 1, c2b, r_y[c, 1, :, H2:W2], r_h2[c, 1])
        rs_push(c, "m2+", ps.at[c, 3, :, c2], r_m2.at[c, 0], at_x(1))
        rs_push(c, "m2-", ps.at[c, 1, :, c2], r_m2.at[c, 1], at_x(3))

    def r3(c):
        for name in ("m10+", "m10-", "t", "m2+", "m2-"):
            rs[c][name].wait_recv()
        fin[:, c1] = (
            ps[c, 0, :, c1].astype(F32) + r_m1[c, 0, 0].astype(F32)
            + r_m1[c, 0, 1].astype(F32) + r_t[c].astype(F32)
        ).astype(BF16)
        fin[:, c2] = (
            ps[c, 0, :, c2].astype(F32) + r_y[c, 0].astype(F32)
            + r_m2[c, 0].astype(F32) + r_m2[c, 1].astype(F32)
        ).astype(BF16)
        acc = jnp.zeros((M, QW), F32)
        for quarter in range(4):
            acc += jnp.dot(
                perm((M, R), 1, quarter), fin[:, quarter * QW : (quarter + 1) * QW],
                preferred_element_type=F32,
            )
        ret_out[c * M : (c + 1) * M, :] = acc.astype(BF16)
        for k in range(max(1, c * SEND), (c + 1) * SEND):
            at = slice(k * 16, (k + 1) * 16)
            pltpu.make_async_remote_copy(
                src_ref=ret_out.at[at], dst_ref=ret_in.at[at], send_sem=s_ret.at[c],
                recv_sem=r_ret.at[c], device_id=at_ep(k, -1), device_id_type=MESH,
            ).start()
        if c == 0:
            ret_in[0:16, :] = ret_out[0:16, :]

    stages = (a0, a1, a2, r0, r1, r2, r3)
    heads = 0
    for step in range(NC + len(stages) - 1):
        for c in range(NC):
            if 0 <= step - c < len(stages):
                stage = stages[step - c]
                if stage is r0 and c == 0:
                    for cp in local[3:]:
                        cp.wait()
                stage(c)
        if step == 1:
            forward_keys()
        if step == 3:
            attend_start()
        if step >= 3 and heads < HK:
            attend(heads, 2)
            heads += 2
    if heads < HK:
        attend(heads, HK - heads)

    col_slot, col_quarter = slot_of(iota((TOK, NEP * 16), 1))
    mine = col_slot.astype(F32) == slot_col
    for c in range(NC):
        wait_messages(ret_in, r_ret, c)
    for quarter in range(4):
        gather = (mine & (col_quarter == quarter)).astype(F32).astype(BF16)
        moe_ref[:, quarter * QW : (quarter + 1) * QW] = jnp.dot(
            gather, ret_in[...], preferred_element_type=F32
        ).astype(BF16)

    for cp in sent:
        cp.wait_send()
    for c in range(NC):
        wait_messages(out_msg, s_a2a, c)
        wait_messages(ret_out, s_ret, c)


def on_device(queries, keys, values, doc_lengths, hidden, norm_gain, token_ids, expert_table, w_gate, w_up, w_down):
    vmem = pl.BlockSpec(memory_space=pltpu.VMEM)
    hbm = pl.BlockSpec(memory_space=pl.ANY)
    dma = pltpu.SemaphoreType.DMA
    attended, moe = pl.pallas_call(
        layer_kernel,
        out_shape=(
            jax.ShapeDtypeStruct((TOK, HQ * HD), BF16),
            jax.ShapeDtypeStruct((TOK, D), BF16),
        ),
        in_specs=[pl.BlockSpec(memory_space=pltpu.SMEM)] + [vmem] * 4 + [hbm] * 6,
        out_specs=(vmem, vmem),
        scratch_shapes=[
            pltpu.VMEM((TOK, HQ * HD), BF16),
            pltpu.VMEM((5, 2, TOK, HK * HD), BF16),
            pltpu.VMEM((TOK, WIN), F32),
            pltpu.VMEM((2 * FB, D), BF16),
            pltpu.VMEM((FB, D), BF16),
            pltpu.VMEM((TOK, D), BF16),
            pltpu.VMEM((4, NEP * 16, TOK), BF16),
            pltpu.VMEM((NEP * 16, QW), BF16),
            pltpu.VMEM((NEP * 16, QW), BF16),
            pltpu.VMEM((NEP * 16, QW), BF16),
            pltpu.VMEM((NEP * 16, QW), BF16),
            pltpu.VMEM((NC, 8, R, D), BF16),
            pltpu.VMEM((NC, 8, R, D), BF16),
            pltpu.VMEM((NC, 4, R, W2), BF16),
            pltpu.VMEM((NC, 2, 2, R, H1), BF16),
            pltpu.VMEM((NC, 2, 2, R, W1), BF16),
            pltpu.VMEM((NC, R, W1), BF16),
            pltpu.VMEM((NC, 2, R, H2), BF16),
            pltpu.VMEM((NC, 2, R, W2), BF16),
            pltpu.VMEM((R, D), BF16),
            dma((6,)),
            dma((6,)),
            dma((6,)),
            dma((NC,)),
            dma((NC,)),
            dma((NC,)),
            dma((NC,)),
            dma((NC, 12)),
            dma((NC, 12)),
            dma((NC, 14)),
            dma((NC, 14)),
        ],
        compiler_params=pltpu.CompilerParams(
            collective_id=0, has_side_effects=True, vmem_limit_bytes=62 * 2**20
        ),
        name="layer",
    )(
        doc_lengths,
        token_ids.reshape(1, TOK),
        expert_table.reshape(VROWS, 128),
        norm_gain.astype(F32).reshape(1, D),
        hidden.reshape(TOK, D),
        queries.reshape(TOK, HQ * HD),
        keys.reshape(TOK, HK * HD),
        values.reshape(TOK, HK * HD),
        w_gate.reshape(FB, D),
        w_up.reshape(FB, D),
        w_down.reshape(FB, D),
    )
    return attended[:, None, :], moe[:, None, :]


def solution(mesh):
    return jax.shard_map(
        on_device,
        mesh=mesh,
        in_specs=(
            P("blk", "ep", None),
            P("blk", "ep", None),
            P("blk", "ep", None),
            P("ep", None),
            P("blk", "ep", None),
            P(),
            P("blk", "ep"),
            P(),
            P("ep", "blk", None),
            P("ep", "blk", None),
            P("ep", "blk", None),
        ),
        out_specs=(P("blk", "ep", None), P("blk", "ep", None)),
        check_vma=False,
    )
```

```python
import functools
import math

import jax
import jax.numpy as jnp
from jax import lax
from jax.experimental import pallas as pl
from jax.experimental.pallas import tpu as pltpu
from jax.sharding import PartitionSpec as P

HQ = 48
HK = 8
HD = 128
GROUPS = HQ // HK
D = 5120
FB = 192
TOK = 128
CAP = 4
NX, NH, NZ = 4, 2, 8
NEP = 32
VROWS = 1184
QW = D // 4

NC = 4
SEND = NEP // NC
R = SEND * CAP
RH = R // 2
M = SEND * 16
MH = M // 2
Z_ORDER = (1, 7, 3, 5, 6, 4, 0, 2)
PZ = NZ // NC
OWN = (Z_ORDER.index(0) // PZ) * SEND + (Z_ORDER.index(0) % PZ) * 2
HALF = 2176
W1 = 1024
W2 = D - W1
H1, H2 = W1 // 2, W2 // 2
ORDER = (
    ("A0", 0), ("A1b", 0), ("K1", 0), ("A0", 1), ("A1a", 0), ("A1c", 0), ("A2b", 0), ("A0", 2),
    ("A1a", 1), ("A0", 3), ("A1c", 1), ("A2a", 0), ("AT", 0), ("AT", 1), ("A1b", 1), ("A1a", 2),
    ("AT", 2), ("A1c", 2), ("AT", 3), ("A2a", 1), ("A1b", 2), ("A1a", 3), ("A1b", 3), ("A1c", 3),
    ("R0", 0), ("A2b", 1), ("A2a", 2), ("A2b", 2), ("A2a", 3), ("A2b", 3), ("R1a", 0), ("R1b", 0),
    ("R0", 1), ("R1c", 0), ("R0", 2), ("R2b", 0), ("R2c", 0), ("R1a", 1), ("R0", 3), ("R2a", 0),
    ("R1b", 1), ("R1a", 2), ("R1b", 2), ("R1c", 1), ("R2c", 1), ("R1a", 3), ("R1b", 3), ("R1c", 2),
    ("R3", 0), ("R2b", 1), ("R2c", 2), ("R2b", 2), ("R2a", 1), ("R1c", 3), ("R2c", 3), ("R2b", 3),
    ("R2a", 2), ("R3", 1), ("R2a", 3), ("R3", 2), ("R3", 3),
)
WIN = 5 * TOK
BLOCK_BACK = (0, 2, 4, 1, 3)

F32 = jnp.float32
BF16 = jnp.bfloat16
MESH = pl.DeviceIdType.MESH


def route(k):
    j = k % SEND
    return Z_ORDER[(k // SEND) * PZ + (j // 2) % PZ], j // (SEND // 2), j % 2


def iota(shape, dim):
    return lax.broadcasted_iota(jnp.int32, shape, dim)


def layer_kernel(
    doc_ref, tok_ref, gain_ref, table_hbm, hid_hbm, q_hbm, k_hbm, v_hbm, wg_hbm, wu_hbm, wd_hbm,
    attn_hbm, moe_hbm,
    table_ref, hid_ref, q_ref, attn_ref, moe_ref,
    kv, bias, wgu, wd, gain, normed, spread, out_msg, in_msg, in_msg2, ret_out, ret_out2, ret_in, ret_in2,
    xs, ps, r_a, r_b, r_y, r_m, r_m0, r_h2, r_m2, r_t, fin, fin2,
    s_loc, s_kv, r_kv, s_a2a, r_a2a, s_a2a2, r_a2a2, s_ret, r_ret, s_ret2, r_ret2, s_ag, r_ag, s_rs, r_rs,
):
    b = lax.axis_index("blk")
    e = lax.axis_index("ep")
    x, h = b // 2, b % 2
    z, yl, core = e // 4, (e // 2) % 2, e % 2
    b_other = x * 2 + (h + 1) % 2

    def at_x(step):
        return (((x + step) % NX) * 2 + h, e)

    at_y = (b_other, e)

    def at_ep(k, sign, blk):
        dz, fy, dc = route(k)
        zz = (z + (dz if sign > 0 else NZ - dz)) % NZ
        return (blk, (zz * 2 + (yl + fy) % 2) * 2 + (core + dc) % 2)

    barrier = pltpu.get_barrier_semaphore()
    far = [k for k in range(NEP) if route(k)[1] == 1]
    peers = [at_x(1), at_x(2), at_x(3), at_y]
    peers += [at_ep(k, 1, b) for k in range(NEP) if k != OWN]
    peers += [at_ep(k, 1, b_other) for k in far]
    for peer in peers:
        pl.semaphore_signal(barrier, inc=1, device_id=peer, device_id_type=MESH)

    local = []
    for i, (src, dst) in enumerate(
        (
            (hid_hbm, hid_ref),
            (table_hbm, table_ref),
            (k_hbm, kv.at[0, 0]),
            (v_hbm, kv.at[0, 1]),
            (wg_hbm, wgu.at[0:FB]),
            (wu_hbm, wgu.at[FB : 2 * FB]),
            (wd_hbm, wd),
            (q_hbm, q_ref),
        )
    ):
        cp = pltpu.make_async_copy(src, dst, s_loc.at[i])
        cp.start()
        local.append(cp)

    for j in range(D // 128):
        gain[:, j * 128 : (j + 1) * 128] = jnp.broadcast_to(gain_ref[j : j + 1, :].astype(F32), (16, 128))

    sent = []

    def push(src, dst, send_sem, recv_sem, device):
        cp = pltpu.make_async_remote_copy(
            src_ref=src, dst_ref=dst, send_sem=send_sem, recv_sem=recv_sem,
            device_id=device, device_id_type=MESH,
        )
        cp.start()
        sent.append(cp)
        return cp

    local[0].wait()

    def norm_rows(i, carry):
        rows = pl.ds(pl.multiple_of(i * 16, 16), 16)
        wide = hid_ref[rows, :].astype(F32)
        scale = lax.rsqrt(jnp.sum(wide * wide, axis=1, keepdims=True) * (1.0 / D) + 1e-05)
        out = (wide * scale * gain[...]).astype(BF16)
        for quarter in range(4):
            at = pl.ds(pl.multiple_of(quarter * TOK + i * 16, 16), 16)
            normed[at, :] = out[:, quarter * QW : (quarter + 1) * QW]
        return carry

    lax.fori_loop(0, TOK // 16, norm_rows, 0)

    pl.semaphore_wait(barrier, len(peers))

    kv_in = [
        push(src, kv.at[step, i], s_kv.at[step * 2 - 2 + i], r_kv.at[step * 2 - 2 + i], at_x(step))
        for step in (1, 2)
        for i, src in ((0, k_hbm), (1, v_hbm))
    ]

    local[1].wait()
    eye = iota((TOK, TOK), 0) == iota((TOK, TOK), 1)
    lane = iota((TOK, TOK), 1)
    tok = tok_ref[...]
    tok_hi, tok_lo = (tok // 128).astype(F32), (tok % 128).astype(F32)
    hi_col = jnp.sum(jnp.where(eye, tok_hi, 0.0), axis=1, keepdims=True)
    lo_col = jnp.sum(jnp.where(eye, tok_lo, 0.0), axis=1, keepdims=True)
    pick = (iota((TOK, VROWS), 1).astype(F32) == hi_col).astype(F32).astype(BF16)
    row = jnp.dot(pick, table_ref[...].astype(F32).astype(BF16), preferred_element_type=F32)
    expert = jnp.sum(jnp.where(lane.astype(F32) == lo_col, row, 0.0), axis=1, keepdims=True)
    onehot = (lane.astype(F32) == expert).astype(F32)
    earlier = (lane < iota((TOK, TOK), 0)).astype(F32).astype(BF16)
    before = jnp.dot(earlier, onehot.astype(BF16), preferred_element_type=F32)
    rank = jnp.sum(before * onehot, axis=1, keepdims=True)
    slot_col = jnp.where(rank < CAP, expert * CAP + rank, -1.0)
    slot_row = jnp.sum(jnp.where(eye, slot_col, 0.0), axis=0, keepdims=True)

    def slot_of(k, i):
        j = k % SEND
        pos = (k // SEND) * PZ + (j // 2) % PZ
        dz = jnp.zeros_like(k)
        for p in range(NZ):
            dz = jnp.where(pos == p, Z_ORDER[p], dz)
        other = (((z + dz) % NZ) * 2 + (yl + j // (SEND // 2)) % 2) * 2 + (core + j % 2) % 2
        return (other * CAP + i % 4).astype(F32), (i // 4) % 4

    msg = iota((NEP * 16, TOK), 0)
    msg_slot, msg_quarter = slot_of(msg // 16, msg)
    here = msg_slot == slot_row
    for quarter in range(4):
        spread[:, quarter * TOK : (quarter + 1) * TOK] = (
            (here & (msg_quarter == quarter)).astype(F32).astype(BF16)
        )

    def spread_columns(n, carry):
        cols = pl.ds(pl.multiple_of(n * 256, 128), 256)
        out_msg[:, cols] = jnp.dot(
            spread[...], normed[:, cols], preferred_element_type=F32
        ).astype(BF16)
        return carry

    lax.fori_loop(0, QW // 256, spread_columns, 0)

    def message(src, dst, send_sem, recv_sem, device):
        pltpu.make_async_remote_copy(
            src_ref=src, dst_ref=dst, send_sem=send_sem, recv_sem=recv_sem,
            device_id=device, device_id_type=MESH,
        ).start()

    def far_at(k):
        start = (k // SEND) * MH + (k % SEND - SEND // 2) * 16
        return slice(start, start + 16)

    def near_at(k):
        return slice(k * 16, (k + 1) * 16)

    for k in range(NEP):
        c = k // SEND
        at = near_at(k)
        if k == OWN:
            in_msg[at, :] = out_msg[at, :]
        else:
            message(out_msg.at[at], in_msg.at[at], s_a2a.at[c], r_a2a.at[c], at_ep(k, 1, b))
        if k in far:
            message(
                out_msg.at[at], in_msg2.at[far_at(k)], s_a2a2.at[c], r_a2a2.at[c], at_ep(k, 1, b_other)
            )

    def wait_part(part, sem):
        pltpu.make_async_copy(part, part, sem).wait()

    def wait_messages(ref, sem, c):
        if c == OWN // SEND:
            first = OWN * 16
            wait_part(ref.at[first + 16 : (c + 1) * M], sem.at[c])
        else:
            wait_part(ref.at[c * M : (c + 1) * M], sem.at[c])

    last = 0
    ends = []
    for i in range(8):
        last = last + doc_ref[0, i]
        ends.append(last)
    q_pos = b * TOK + iota((TOK, TOK), 0)
    start = jnp.zeros((TOK, TOK), jnp.int32)
    for end in ends:
        start = jnp.where(q_pos >= end, end, start)
    for s, back in enumerate(BLOCK_BACK):
        k_pos = (b - back) * TOK + iota((TOK, TOK), 1)
        allowed = (k_pos >= start) & (k_pos <= q_pos)
        bias[:, s * TOK : (s + 1) * TOK] = jnp.where(allowed, 0.0, -1e30).astype(F32)

    kv_fwd = []

    def forward_keys():
        for cp in kv_in:
            cp.wait_recv()
        local[2].wait()
        local[3].wait()
        for i in range(2):
            kv_fwd.append(push(kv.at[h + i], kv.at[3 + i], s_kv.at[4 + i], r_kv.at[4 + i], at_y))

    def attend_start():
        for cp in kv_fwd:
            cp.wait_recv()
        local[7].wait()

    def attend(first, count):
        def one(g, carry):
            head = pl.ds(pl.multiple_of(g * HD, HD), HD)
            wide = pl.ds(pl.multiple_of(g * GROUPS * HD, HD), GROUPS * HD)
            keys = kv[:, 0, :, head].reshape(WIN, HD)
            vals = kv[:, 1, :, head].reshape(WIN, HD)
            q_all = q_ref[:, wide]
            outs = []
            for i in range(GROUPS):
                q_one = q_all[:, i * HD : (i + 1) * HD]
                score = lax.dot_general(
                    q_one, keys, (((1,), (1,)), ((), ())), preferred_element_type=F32
                ) + bias[...]
                top = jnp.max(score, axis=1, keepdims=True)
                weight = jnp.exp((score - top) * (1.0 / math.sqrt(HD)))
                total = jnp.sum(weight, axis=1, keepdims=True)
                mixed = jnp.dot(weight.astype(BF16), vals, preferred_element_type=F32)
                outs.append((mixed / total).astype(BF16))
            attn_ref[:, wide] = jnp.concatenate(outs, axis=1)
            return carry

        lax.fori_loop(first, first + count, one, 0)

    def perm(shape, row_dim, quarter):
        rr, mm = iota(shape, row_dim), iota(shape, 1 - row_dim)
        same = (mm // 16 == rr // 4) & ((mm // 4) % 4 == quarter) & (mm % 4 == rr % 4)
        return same.astype(F32).astype(BF16)

    ag = [dict() for _ in range(NC)]
    rs = [dict() for _ in range(NC)]

    def ag_push(c, name, src, dst, device):
        i = len(ag[c])
        ag[c][name] = push(src, dst, s_ag.at[c, i], r_ag.at[c, i], device)

    def rs_push(c, name, src, dst, device):
        i = len(rs[c])
        rs[c][name] = push(src, dst, s_rs.at[c, i], r_rs.at[c, i], device)

    def ag_wait(c, *names):
        for name in names:
            ag[c][name].wait_recv()

    def rs_wait(c, *names):
        for name in names:
            rs[c][name].wait_recv()

    every, lo, hi = slice(0, D), slice(0, HALF), slice(HALF, D)
    c1, c2 = slice(0, W1), slice(W1, D)
    c1a, c1b = slice(0, H1), slice(H1, W1)
    c2a, c2b = slice(W1, W1 + H2), slice(W1 + H2, D)
    allr, near, away = slice(0, R), slice(0, RH), slice(RH, R)

    def a0(c):
        wait_messages(in_msg, r_a2a, c)
        wait_part(in_msg2.at[c * MH : (c + 1) * MH], r_a2a2.at[c])
        for quarter in range(4):
            cols = slice(quarter * QW, (quarter + 1) * QW)
            xs[c, 0, :, cols] = jnp.dot(
                perm((R, M), 0, quarter), in_msg[c * M : (c + 1) * M, :], preferred_element_type=F32
            ).astype(BF16)
            xs[c, 4, away, cols] = jnp.dot(
                perm((RH, MH), 0, quarter), in_msg2[c * MH : (c + 1) * MH, :], preferred_element_type=F32
            ).astype(BF16)
        ag_push(c, "1", xs.at[c, 0], xs.at[c, 1], at_x(1))
        ag_push(c, "3", xs.at[c, 0], xs.at[c, 3], at_x(3))
        ag_push(c, "4", xs.at[c, 0, near], xs.at[c, 4, near], at_y)
        ag_push(c, "5f", xs.at[c, 4, away], xs.at[c, 5, away], at_x(1))
        ag_push(c, "7f", xs.at[c, 4, away], xs.at[c, 7, away], at_x(3))

    def hop(c, name, i, j, rows, cols, device):
        ag_push(c, name, xs.at[c, i, rows, cols], xs.at[c, j, rows, cols], device)

    def a1a(c):
        ag_wait(c, "1", "3")
        hop(c, "2a", 1, 2, allr, lo, at_x(1))
        hop(c, "2b", 3, 2, allr, hi, at_x(3))
        hop(c, "5y", 1, 5, near, c2, at_y)
        hop(c, "7y", 3, 7, near, c2, at_y)

    def a1b(c):
        ag_wait(c, "4")
        hop(c, "5x", 4, 5, near, c1, at_x(1))
        hop(c, "7x", 4, 7, near, c1, at_x(3))

    def a1c(c):
        ag_wait(c, "5f", "7f")
        hop(c, "6fa", 5, 6, away, lo, at_x(1))
        hop(c, "6fb", 7, 6, away, hi, at_x(3))

    def a2a(c):
        ag_wait(c, "2a", "2b")
        hop(c, "6y", 2, 6, near, c2, at_y)

    def a2b(c):
        ag_wait(c, "5x", "7x")
        hop(c, "6a", 5, 6, near, c1a, at_x(1))
        hop(c, "6b", 7, 6, near, c1b, at_x(3))

    def r0(c):
        ag_wait(c, "5y", "7y", "6fa", "6fb", "6a", "6b", "6y")
        rows = xs[c].reshape(8 * R, D)
        both = lax.dot_general(
            rows, wgu[...], (((1,), (1,)), ((), ())), preferred_element_type=F32
        )
        gate, up = both[:, :FB], both[:, FB:]
        act = (gate / (1.0 + jnp.exp(-gate)) * up).astype(BF16)

        def down(n, carry):
            cols = pl.ds(pl.multiple_of(n * 512, 128), 512)
            res = jnp.dot(act, wd[:, cols], preferred_element_type=F32).astype(BF16)
            ps[c, :, :, cols] = res.reshape(8, R, 512)
            return carry

        lax.fori_loop(0, D // 512, down, 0)
        rs_push(c, "y", ps.at[c, 4:8, near, c2], r_y.at[c], at_y)
        for dh in range(2):
            rs_push(c, "a%d+" % dh, ps.at[c, dh * 4 + 2, away, lo], r_a.at[c, dh, :, lo], at_x(1))
            rs_push(c, "a%d-" % dh, ps.at[c, dh * 4 + 2, away, hi], r_a.at[c, dh, :, hi], at_x(3))
            rs_push(c, "b%d+" % dh, ps.at[c, dh * 4 + 2, near, c1a], r_b.at[c, dh, :, c1a], at_x(1))
            rs_push(c, "b%d-" % dh, ps.at[c, dh * 4 + 2, near, c1b], r_b.at[c, dh, :, c1b], at_x(3))

    def add(c, i, rows, cols, *terms):
        total = ps[c, i, rows, cols].astype(F32)
        for term in terms:
            total = total + term.astype(F32)
        return total.astype(BF16)

    def grow(c, i, rows, cols, *terms):
        ps[c, i, rows, cols] = add(c, i, rows, cols, *terms)

    def r1a(c):
        for dh in range(2):
            plus, minus = dh * 4 + 3, dh * 4 + 1
            rs_wait(c, "a%d+" % dh, "a%d-" % dh)
            grow(c, plus, away, lo, r_a[c, dh, :, lo])
            grow(c, minus, away, hi, r_a[c, dh, :, hi])
            rs_push(c, "m%d+" % dh, ps.at[c, plus, away], r_m.at[c, dh, 0], at_x(1))
            rs_push(c, "m%d-" % dh, ps.at[c, minus, away], r_m.at[c, dh, 1], at_x(3))

    def r1b(c):
        for dh in range(2):
            plus, minus = dh * 4 + 3, dh * 4 + 1
            rs_wait(c, "b%d+" % dh, "b%d-" % dh)
            grow(c, plus, near, c1a, r_b[c, dh, :, c1a])
            grow(c, minus, near, c1b, r_b[c, dh, :, c1b])
            rs_push(c, "n%d+" % dh, ps.at[c, plus, near, c1], r_m0.at[c, dh, 0], at_x(1))
            rs_push(c, "n%d-" % dh, ps.at[c, minus, near, c1], r_m0.at[c, dh, 1], at_x(3))

    def r1c(c):
        rs_wait(c, "y")
        grow(c, 2, near, c2, r_y[c, 2])
        rs_push(c, "h+", ps.at[c, 2, near, c2a], r_h2.at[c, :, 0:H2], at_x(1))
        rs_push(c, "h-", ps.at[c, 2, near, c2b], r_h2.at[c, :, H2:W2], at_x(3))

    def send_back(c, j, src, dst, at, send_sem, recv_sem, blk):
        k = c * SEND + j
        if k == OWN:
            dst[at, :] = src[at, :]
        else:
            message(src.at[at], dst.at[at], send_sem.at[c], recv_sem.at[c], at_ep(k, -1, blk))

    def to_messages(rows):
        acc = jnp.zeros((MH, QW), F32)
        for quarter in range(4):
            acc += jnp.dot(
                perm((MH, RH), 1, quarter), rows[:, quarter * QW : (quarter + 1) * QW],
                preferred_element_type=F32,
            )
        return acc.astype(BF16)

    def r2a(c):
        rs_wait(c, "h+", "h-")
        for i, a in ((3, 0), (1, 1)):
            for half, cols in enumerate((c2a, c2b)):
                part = slice(half * H2, (half + 1) * H2)
                terms = [r_y[c, i, :, part]]
                if half == a:
                    terms.append(r_h2[c, :, part])
                ps[c, i, near, cols] = add(c, i, near, cols, *terms)
        rs_push(c, "k+", ps.at[c, 3, near, c2], r_m2.at[c, 0], at_x(1))
        rs_push(c, "k-", ps.at[c, 1, near, c2], r_m2.at[c, 1], at_x(3))

    def r2b(c):
        rs_wait(c, "n1+", "n1-")
        ps[c, 4, near, c1] = add(c, 4, near, c1, r_m0[c, 1, 0], r_m0[c, 1, 1])
        rs_push(c, "t", ps.at[c, 4, near, c1], r_t.at[c], at_y)

    def r2c(c):
        rs_wait(c, "m0+", "m0-", "m1+", "m1-")
        fin[...] = add(c, 0, away, every, r_m[c, 0, 0], r_m[c, 0, 1])
        fin2[...] = add(c, 4, away, every, r_m[c, 1, 0], r_m[c, 1, 1])
        ret_out[c * M + MH : (c + 1) * M, :] = to_messages(fin)
        ret_out2[c * MH : (c + 1) * MH, :] = to_messages(fin2)
        for j in range(SEND // 2, SEND):
            k = c * SEND + j
            send_back(c, j, ret_out, ret_in, near_at(k), s_ret, r_ret, b)
            send_back(c, j, ret_out2, ret_in2, far_at(k), s_ret2, r_ret2, b_other)

    def r3(c):
        rs_wait(c, "n0+", "n0-", "t", "k+", "k-")
        fin[:, c1] = add(c, 0, near, c1, r_m0[c, 0, 0], r_m0[c, 0, 1], r_t[c])
        fin[:, c2] = add(c, 0, near, c2, r_y[c, 0], r_m2[c, 0], r_m2[c, 1])
        ret_out[c * M : c * M + MH, :] = to_messages(fin)
        for j in range(SEND // 2):
            send_back(c, j, ret_out, ret_in, near_at(c * SEND + j), s_ret, r_ret, b)

    def k1(c):
        forward_keys()

    def at(c):
        if c == 0:
            attend_start()
        attend(2 * c, 2)

    def r0_first(c):
        if c == 0:
            for cp in local[4:7]:
                cp.wait()
        r0(c)

    attn_out = pltpu.make_async_copy(attn_ref, attn_hbm, s_loc.at[8])
    pieces = dict(
        A0=a0, A1a=a1a, A1b=a1b, A1c=a1c, A2a=a2a, A2b=a2b, R0=r0_first,
        R1a=r1a, R1b=r1b, R1c=r1c, R2a=r2a, R2b=r2b, R2c=r2c, R3=r3, K1=k1, AT=at,
    )
    for name, c in ORDER:
        pieces[name](c)
    attn_out.start()

    def collect(shape, k, i):
        col_slot, col_quarter = slot_of(k, i)
        return col_slot == slot_col, col_quarter

    i1, i2 = iota((TOK, NEP * 16), 1), iota((TOK, NEP * 8), 1)
    mine1, quarter1 = collect((TOK, NEP * 16), i1 // 16, i1)
    mine2, quarter2 = collect((TOK, NEP * 8), (i2 // MH) * SEND + SEND // 2 + (i2 % MH) // 16, i2)
    for c in range(NC):
        wait_messages(ret_in, r_ret, c)
        wait_part(ret_in2.at[c * MH : (c + 1) * MH], r_ret2.at[c])
    for quarter in range(4):
        gather1 = (mine1 & (quarter1 == quarter)).astype(F32).astype(BF16)
        gather2 = (mine2 & (quarter2 == quarter)).astype(F32).astype(BF16)
        moe_ref[:, quarter * QW : (quarter + 1) * QW] = (
            jnp.dot(gather1, ret_in[...], preferred_element_type=F32)
            + jnp.dot(gather2, ret_in2[...], preferred_element_type=F32)
        ).astype(BF16)
    moe_out = pltpu.make_async_copy(moe_ref, moe_hbm, s_loc.at[9])
    moe_out.start()

    for cp in sent:
        cp.wait_send()
    for c in range(NC):
        wait_messages(out_msg, s_a2a, c)
        wait_part(in_msg2.at[c * MH : (c + 1) * MH], s_a2a2.at[c])
        wait_messages(ret_out, s_ret, c)
        wait_part(ret_out2.at[c * MH : (c + 1) * MH], s_ret2.at[c])
    attn_out.wait()
    moe_out.wait()


def on_device(queries, keys, values, doc_lengths, hidden, norm_gain, token_ids, expert_table, w_gate, w_up, w_down):
    vmem = pl.BlockSpec(memory_space=pltpu.VMEM)
    hbm = pl.BlockSpec(memory_space=pl.ANY)
    dma = pltpu.SemaphoreType.DMA
    attended, moe = pl.pallas_call(
        layer_kernel,
        out_shape=(
            jax.ShapeDtypeStruct((TOK, HQ * HD), BF16),
            jax.ShapeDtypeStruct((TOK, D), BF16),
        ),
        in_specs=[pl.BlockSpec(memory_space=pltpu.SMEM)] + [vmem] * 2 + [hbm] * 8,
        out_specs=(hbm, hbm),
        scratch_shapes=[
            pltpu.VMEM((VROWS, 128), jnp.int32),
            pltpu.VMEM((TOK, D), BF16),
            pltpu.VMEM((TOK, HQ * HD), BF16),
            pltpu.VMEM((TOK, HQ * HD), BF16),
            pltpu.VMEM((TOK, D), BF16),
            pltpu.VMEM((5, 2, TOK, HK * HD), BF16),
            pltpu.VMEM((TOK, WIN), F32),
            pltpu.VMEM((2 * FB, D), BF16),
            pltpu.VMEM((FB, D), BF16),
            pltpu.VMEM((16, D), F32),
            pltpu.VMEM((4 * TOK, QW), BF16),
            pltpu.VMEM((NEP * 16, 4 * TOK), BF16),
            pltpu.VMEM((NEP * 16, QW), BF16),
            pltpu.VMEM((NEP * 16, QW), BF16),
            pltpu.VMEM((NEP * 8, QW), BF16),
            pltpu.VMEM((NEP * 16, QW), BF16),
            pltpu.VMEM((NEP * 8, QW), BF16),
            pltpu.VMEM((NEP * 16, QW), BF16),
            pltpu.VMEM((NEP * 8, QW), BF16),
            pltpu.VMEM((NC, 8, R, D), BF16),
            pltpu.VMEM((NC, 8, R, D), BF16),
            pltpu.VMEM((NC, 2, RH, D), BF16),
            pltpu.VMEM((NC, 2, RH, W1), BF16),
            pltpu.VMEM((NC, 4, RH, W2), BF16),
            pltpu.VMEM((NC, 2, 2, RH, D), BF16),
            pltpu.VMEM((NC, 2, 2, RH, W1), BF16),
            pltpu.VMEM((NC, RH, W2), BF16),
            pltpu.VMEM((NC, 2, RH, W2), BF16),
            pltpu.VMEM((NC, RH, W1), BF16),
            pltpu.VMEM((RH, D), BF16),
            pltpu.VMEM((RH, D), BF16),
            dma((10,)),
            dma((6,)),
            dma((6,)),
            dma((NC,)),
            dma((NC,)),
            dma((NC,)),
            dma((NC,)),
            dma((NC,)),
            dma((NC,)),
            dma((NC,)),
            dma((NC,)),
            dma((NC, 16)),
            dma((NC, 16)),
            dma((NC, 22)),
            dma((NC, 22)),
        ],
        compiler_params=pltpu.CompilerParams(
            collective_id=0, has_side_effects=True, vmem_limit_bytes=62 * 2**20
        ),
        name="layer",
    )(
        doc_lengths,
        token_ids.reshape(1, TOK),
        norm_gain.reshape(D // 128, 128),
        expert_table.reshape(VROWS, 128),
        hidden.reshape(TOK, D),
        queries.reshape(TOK, HQ * HD),
        keys.reshape(TOK, HK * HD),
        values.reshape(TOK, HK * HD),
        w_gate.reshape(FB, D),
        w_up.reshape(FB, D),
        w_down.reshape(FB, D),
    )
    return attended[:, None, :], moe[:, None, :]


def solution(mesh):
    return jax.shard_map(
        on_device,
        mesh=mesh,
        in_specs=(
            P("blk", "ep", None),
            P("blk", "ep", None),
            P("blk", "ep", None),
            P("ep", None),
            P("blk", "ep", None),
            P(),
            P("blk", "ep"),
            P(),
            P("ep", "blk", None),
            P("ep", "blk", None),
            P("ep", "blk", None),
        ),
        out_specs=(P("blk", "ep", None), P("blk", "ep", None)),
        check_vma=False,
    )
```

```python
import functools
import math

import jax
import jax.numpy as jnp
from jax import lax
from jax.experimental import pallas as pl
from jax.experimental.pallas import tpu as pltpu
from jax.sharding import PartitionSpec as P

HQ = 48
HK = 8
HD = 128
GROUPS = HQ // HK
D = 5120
FB = 192
TOK = 128
CAP = 4
NX, NH, NZ = 4, 2, 8
NEP = 32
VROWS = 1184
QW = D // 4

NC = 4
SEND = NEP // NC
R = SEND * CAP
RH = R // 2
M = SEND * 16
MH = M // 2
Z_ORDER = (1, 7, 3, 5, 6, 4, 0, 2)
PZ = NZ // NC
OWN = (Z_ORDER.index(0) // PZ) * SEND + (Z_ORDER.index(0) % PZ) * 2
HALF = 2432
W1 = 1536
W2 = D - W1
H1, H2 = W1 // 2, W2 // 2
KEYS_FIRST = True
MESSAGES_FIRST = 4
ORDER = (
    ("A0", 0), ("A1b", 0), ("K1", 0), ("A0", 1), ("A1a", 0), ("A1c", 0), ("A2b", 0), ("A0", 2),
    ("A1a", 1), ("A0", 3), ("A1c", 1), ("A2a", 0), ("AT", 0), ("AT", 1), ("A1b", 1), ("AT", 2),
    ("A1a", 2), ("A1c", 2), ("AT", 3), ("A2a", 1), ("A1b", 2), ("A1a", 3), ("A1b", 3), ("R0", 0),
    ("A2b", 1), ("A1c", 3), ("A2a", 2), ("A2b", 2), ("A2a", 3), ("A2b", 3), ("R1a", 0), ("R1b", 0),
    ("R0", 1), ("R1c", 0), ("R0", 2), ("R2b", 0), ("R2c", 0), ("R0", 3), ("R2a", 0), ("R1a", 1),
    ("R1b", 1), ("R1c", 1), ("R1a", 2), ("R1b", 2), ("R1a", 3), ("R1b", 3), ("R1c", 2), ("R3", 0),
    ("R2c", 1), ("R2b", 1), ("R2a", 1), ("R1c", 3), ("R2c", 2), ("R2b", 2), ("R2c", 3), ("R2b", 3),
    ("R2a", 2), ("R3", 1), ("R2a", 3), ("R3", 2), ("R3", 3),
)
WIN = 5 * TOK
BLOCK_BACK = (0, 2, 4, 1, 3)

F32 = jnp.float32
BF16 = jnp.bfloat16
MESH = pl.DeviceIdType.MESH


def route(k):
    j = k % SEND
    return Z_ORDER[(k // SEND) * PZ + (j // 2) % PZ], j // (SEND // 2), j % 2


def iota(shape, dim):
    return lax.broadcasted_iota(jnp.int32, shape, dim)


def layer_kernel(
    doc_ref, tok_ref, gain_ref, table_hbm, hid_hbm, q_hbm, k_hbm, v_hbm, wg_hbm, wu_hbm, wd_hbm,
    attn_hbm, moe_hbm,
    table_ref, hid_ref, q_ref, attn_ref, moe_ref,
    kv, bias, wgu, wd, gain, normed, spread, out_msg, in_msg, in_msg2, ret_out, ret_out2, ret_in, ret_in2,
    p_near, p_far, p_back, gath, gath2, acc, xs, ps, r_a, r_b, r_y, r_m, r_m0, r_h2, r_m2, r_t, fin, fin2,
    s_loc, s_kv, r_kv, s_a2a, r_a2a, s_a2a2, r_a2a2, s_ret, r_ret, s_ret2, r_ret2, s_ag, r_ag, s_rs, r_rs,
):
    b = lax.axis_index("blk")
    e = lax.axis_index("ep")
    x, h = b // 2, b % 2
    z, yl, core = e // 4, (e // 2) % 2, e % 2
    b_other = x * 2 + (h + 1) % 2

    def at_x(step):
        return (((x + step) % NX) * 2 + h, e)

    at_y = (b_other, e)

    def at_ep(k, sign, blk):
        dz, fy, dc = route(k)
        zz = (z + (dz if sign > 0 else NZ - dz)) % NZ
        return (blk, (zz * 2 + (yl + fy) % 2) * 2 + (core + dc) % 2)

    barrier = pltpu.get_barrier_semaphore()
    far = [k for k in range(NEP) if route(k)[1] == 1]
    peers = [at_x(1), at_x(2), at_x(3), at_y]
    peers += [at_ep(k, 1, b) for k in range(NEP) if k != OWN]
    peers += [at_ep(k, 1, b_other) for k in far]
    for peer in peers:
        pl.semaphore_signal(barrier, inc=1, device_id=peer, device_id_type=MESH)

    local = []
    for i, (src, dst) in enumerate(
        (
            (hid_hbm, hid_ref),
            (table_hbm, table_ref),
            (k_hbm, kv.at[0, 0]),
            (v_hbm, kv.at[0, 1]),
            (wg_hbm, wgu.at[0:FB]),
            (wu_hbm, wgu.at[FB : 2 * FB]),
            (wd_hbm, wd),
            (q_hbm, q_ref),
        )
    ):
        cp = pltpu.make_async_copy(src, dst, s_loc.at[i])
        cp.start()
        local.append(cp)

    for j in range(D // 128):
        gain[:, j * 128 : (j + 1) * 128] = jnp.broadcast_to(gain_ref[j : j + 1, :].astype(F32), (16, 128))

    sent = []

    def push(src, dst, send_sem, recv_sem, device):
        cp = pltpu.make_async_remote_copy(
            src_ref=src, dst_ref=dst, send_sem=send_sem, recv_sem=recv_sem,
            device_id=device, device_id_type=MESH,
        )
        cp.start()
        sent.append(cp)
        return cp

    local[0].wait()

    def norm_rows(i, carry):
        rows = pl.ds(pl.multiple_of(i * 16, 16), 16)
        wide = hid_ref[rows, :].astype(F32)
        scale = lax.rsqrt(jnp.sum(wide * wide, axis=1, keepdims=True) * (1.0 / D) + 1e-05)
        out = (wide * scale * gain[...]).astype(BF16)
        for quarter in range(4):
            at = pl.ds(pl.multiple_of(quarter * TOK + i * 16, 16), 16)
            normed[at, :] = out[:, quarter * QW : (quarter + 1) * QW]
        return carry

    lax.fori_loop(0, TOK // 16, norm_rows, 0)

    pl.semaphore_wait(barrier, len(peers))

    kv_in = []

    def k0(c):
        for i, src in ((0, k_hbm), (1, v_hbm)):
            kv_in.append(
                push(src, kv.at[c + 1, i], s_kv.at[2 * c + i], r_kv.at[2 * c + i], at_x(c + 1))
            )

    if KEYS_FIRST:
        k0(0)
        k0(1)

    local[1].wait()
    eye = iota((TOK, TOK), 0) == iota((TOK, TOK), 1)
    lane = iota((TOK, TOK), 1)
    tok = tok_ref[...]
    tok_hi, tok_lo = (tok // 128).astype(F32), (tok % 128).astype(F32)
    hi_col = jnp.sum(jnp.where(eye, tok_hi, 0.0), axis=1, keepdims=True)
    lo_col = jnp.sum(jnp.where(eye, tok_lo, 0.0), axis=1, keepdims=True)
    pick = (iota((TOK, VROWS), 1).astype(F32) == hi_col).astype(F32).astype(BF16)
    row = jnp.dot(pick, table_ref[...].astype(F32).astype(BF16), preferred_element_type=F32)
    expert = jnp.sum(jnp.where(lane.astype(F32) == lo_col, row, 0.0), axis=1, keepdims=True)
    onehot = (lane.astype(F32) == expert).astype(F32)
    earlier = (lane < iota((TOK, TOK), 0)).astype(F32).astype(BF16)
    before = jnp.dot(earlier, onehot.astype(BF16), preferred_element_type=F32)
    rank = jnp.sum(before * onehot, axis=1, keepdims=True)
    slot_col = jnp.where(rank < CAP, expert * CAP + rank, -1.0)
    slot_row = jnp.sum(jnp.where(eye, slot_col, 0.0), axis=0, keepdims=True)

    def slot_of(k, i):
        j = k % SEND
        pos = (k // SEND) * PZ + (j // 2) % PZ
        dz = jnp.zeros_like(k)
        for p in range(NZ):
            dz = jnp.where(pos == p, Z_ORDER[p], dz)
        other = (((z + dz) % NZ) * 2 + (yl + j // (SEND // 2)) % 2) * 2 + (core + j % 2) % 2
        return (other * CAP + i % 4).astype(F32), (i // 4) % 4

    msg = iota((NEP * 16, TOK), 0)
    msg_slot, msg_quarter = slot_of(msg // 16, msg)
    here = msg_slot == slot_row
    for quarter in range(4):
        spread[:, quarter * TOK : (quarter + 1) * TOK] = (
            (here & (msg_quarter == quarter)).astype(F32).astype(BF16)
        )

    def spread_columns(n, carry):
        cols = pl.ds(pl.multiple_of(n * 256, 128), 256)
        out_msg[:, cols] = jnp.dot(
            spread[...], normed[:, cols], preferred_element_type=F32
        ).astype(BF16)
        return carry

    lax.fori_loop(0, QW // 256, spread_columns, 0)

    def message(src, dst, send_sem, recv_sem, device):
        pltpu.make_async_remote_copy(
            src_ref=src, dst_ref=dst, send_sem=send_sem, recv_sem=recv_sem,
            device_id=device, device_id_type=MESH,
        ).start()

    def far_at(k):
        start = (k // SEND) * MH + (k % SEND - SEND // 2) * 16
        return slice(start, start + 16)

    def near_at(k):
        return slice(k * 16, (k + 1) * 16)

    def m(c):
        for k in range(c * SEND, (c + 1) * SEND):
            at = near_at(k)
            if k == OWN:
                in_msg[at, :] = out_msg[at, :]
            else:
                message(out_msg.at[at], in_msg.at[at], s_a2a.at[c], r_a2a.at[c], at_ep(k, 1, b))
            if k in far:
                message(
                    out_msg.at[at], in_msg2.at[far_at(k)], s_a2a2.at[c], r_a2a2.at[c],
                    at_ep(k, 1, b_other),
                )

    for c in range(MESSAGES_FIRST):
        m(c)

    def wait_part(part, sem):
        pltpu.make_async_copy(part, part, sem).wait()

    def wait_messages(ref, sem, c):
        if c == OWN // SEND:
            first = OWN * 16
            wait_part(ref.at[first + 16 : (c + 1) * M], sem.at[c])
        else:
            wait_part(ref.at[c * M : (c + 1) * M], sem.at[c])

    last = 0
    ends = []
    for i in range(8):
        last = last + doc_ref[0, i]
        ends.append(last)
    q_pos = b * TOK + iota((TOK, TOK), 0)
    start = jnp.zeros((TOK, TOK), jnp.int32)
    for end in ends:
        start = jnp.where(q_pos >= end, end, start)
    for s, back in enumerate(BLOCK_BACK):
        k_pos = (b - back) * TOK + iota((TOK, TOK), 1)
        allowed = (k_pos >= start) & (k_pos <= q_pos)
        bias[:, s * TOK : (s + 1) * TOK] = jnp.where(allowed, 0.0, -1e30).astype(F32)

    kv_fwd = []

    def forward_keys():
        for cp in kv_in:
            cp.wait_recv()
        local[2].wait()
        local[3].wait()
        for i in range(2):
            kv_fwd.append(push(kv.at[h + i], kv.at[3 + i], s_kv.at[4 + i], r_kv.at[4 + i], at_y))

    def attend_start():
        for cp in kv_fwd:
            cp.wait_recv()
        local[7].wait()

    def attend(first, count):
        def one(g, carry):
            head = pl.ds(pl.multiple_of(g * HD, HD), HD)
            wide = pl.ds(pl.multiple_of(g * GROUPS * HD, HD), GROUPS * HD)
            keys = kv[:, 0, :, head].reshape(WIN, HD)
            vals = kv[:, 1, :, head].reshape(WIN, HD)
            q_all = q_ref[:, wide]
            outs = []
            for i in range(GROUPS):
                q_one = q_all[:, i * HD : (i + 1) * HD]
                score = lax.dot_general(
                    q_one, keys, (((1,), (1,)), ((), ())), preferred_element_type=F32
                ) + bias[...]
                top = jnp.max(score, axis=1, keepdims=True)
                weight = jnp.exp((score - top) * (1.0 / math.sqrt(HD)))
                total = jnp.sum(weight, axis=1, keepdims=True)
                mixed = jnp.dot(weight.astype(BF16), vals, preferred_element_type=F32)
                outs.append((mixed / total).astype(BF16))
            attn_ref[:, wide] = jnp.concatenate(outs, axis=1)
            return carry

        lax.fori_loop(first, first + count, one, 0)

    def perm(count, row_dim):
        rr, mm = iota((4 * count, 4 * count), row_dim), iota((4 * count, 4 * count), 1 - row_dim)
        row = rr % count
        same = (mm // 16 == row // 4) & ((mm // 4) % 4 == rr // count) & (mm % 4 == row % 4)
        return same.astype(F32).astype(BF16)

    p_near[...] = perm(R, 0)
    p_far[...] = perm(RH, 0)
    p_back[...] = perm(RH, 1)

    def collect(ref, k, i):
        col_slot, col_quarter = slot_of(k, i)
        mine = col_slot == slot_col
        for quarter in range(4):
            ref[quarter * TOK : (quarter + 1) * TOK, :] = (
                (mine & (col_quarter == quarter)).astype(F32).astype(BF16)
            )

    i1, i2 = iota((TOK, NEP * 16), 1), iota((TOK, NEP * 8), 1)
    collect(gath, i1 // 16, i1)
    collect(gath2, (i2 // MH) * SEND + SEND // 2 + (i2 % MH) // 16, i2)

    ag = [dict() for _ in range(NC)]
    rs = [dict() for _ in range(NC)]

    def ag_push(c, name, src, dst, device):
        i = len(ag[c])
        ag[c][name] = push(src, dst, s_ag.at[c, i], r_ag.at[c, i], device)

    def rs_push(c, name, src, dst, device):
        i = len(rs[c])
        rs[c][name] = push(src, dst, s_rs.at[c, i], r_rs.at[c, i], device)

    def ag_wait(c, *names):
        for name in names:
            ag[c][name].wait_recv()

    def rs_wait(c, *names):
        for name in names:
            rs[c][name].wait_recv()

    every, lo, hi = slice(0, D), slice(0, HALF), slice(HALF, D)
    c1, c2 = slice(0, W1), slice(W1, D)
    c1a, c1b = slice(0, H1), slice(H1, W1)
    c2a, c2b = slice(W1, W1 + H2), slice(W1 + H2, D)
    allr, near, away = slice(0, R), slice(0, RH), slice(RH, R)

    def a0(c):
        wait_messages(in_msg, r_a2a, c)
        wait_part(in_msg2.at[c * MH : (c + 1) * MH], r_a2a2.at[c])
        own = jnp.dot(p_near[...], in_msg[c * M : (c + 1) * M, :], preferred_element_type=F32).astype(BF16)
        two = jnp.dot(p_far[...], in_msg2[c * MH : (c + 1) * MH, :], preferred_element_type=F32).astype(BF16)
        for quarter in range(4):
            cols = slice(quarter * QW, (quarter + 1) * QW)
            xs[c, 0, :, cols] = own[quarter * R : (quarter + 1) * R, :]
            xs[c, 4, away, cols] = two[quarter * RH : (quarter + 1) * RH, :]
        ag_push(c, "1", xs.at[c, 0], xs.at[c, 1], at_x(1))
        ag_push(c, "3", xs.at[c, 0], xs.at[c, 3], at_x(3))
        ag_push(c, "4", xs.at[c, 0, near], xs.at[c, 4, near], at_y)
        ag_push(c, "5f", xs.at[c, 4, away], xs.at[c, 5, away], at_x(1))
        ag_push(c, "7f", xs.at[c, 4, away], xs.at[c, 7, away], at_x(3))

    def hop(c, name, i, j, rows, cols, device):
        ag_push(c, name, xs.at[c, i, rows, cols], xs.at[c, j, rows, cols], device)

    def a1a(c):
        ag_wait(c, "1", "3")
        hop(c, "2a", 1, 2, allr, lo, at_x(1))
        hop(c, "2b", 3, 2, allr, hi, at_x(3))
        hop(c, "5y", 1, 5, near, c2, at_y)
        hop(c, "7y", 3, 7, near, c2, at_y)

    def a1b(c):
        ag_wait(c, "4")
        hop(c, "5x", 4, 5, near, c1, at_x(1))
        hop(c, "7x", 4, 7, near, c1, at_x(3))

    def a1c(c):
        ag_wait(c, "5f", "7f")
        hop(c, "6fa", 5, 6, away, lo, at_x(1))
        hop(c, "6fb", 7, 6, away, hi, at_x(3))

    def a2a(c):
        ag_wait(c, "2a", "2b")
        hop(c, "6y", 2, 6, near, c2, at_y)

    def a2b(c):
        ag_wait(c, "5x", "7x")
        hop(c, "6a", 5, 6, near, c1a, at_x(1))
        hop(c, "6b", 7, 6, near, c1b, at_x(3))

    def r0(c):
        ag_wait(c, "5y", "7y", "6fa", "6fb", "6a", "6b", "6y")
        rows = xs[c].reshape(8 * R, D)
        both = lax.dot_general(
            rows, wgu[...], (((1,), (1,)), ((), ())), preferred_element_type=F32
        )
        gate, up = both[:, :FB], both[:, FB:]
        act = (gate / (1.0 + jnp.exp(-gate)) * up).astype(BF16)

        def down(n, carry):
            cols = pl.ds(pl.multiple_of(n * 512, 128), 512)
            res = jnp.dot(act, wd[:, cols], preferred_element_type=F32).astype(BF16)
            ps[c, :, :, cols] = res.reshape(8, R, 512)
            return carry

        lax.fori_loop(0, D // 512, down, 0)
        rs_push(c, "y", ps.at[c, 4:8, near, c2], r_y.at[c], at_y)
        for dh in range(2):
            rs_push(c, "a%d+" % dh, ps.at[c, dh * 4 + 2, away, lo], r_a.at[c, dh, :, lo], at_x(1))
            rs_push(c, "a%d-" % dh, ps.at[c, dh * 4 + 2, away, hi], r_a.at[c, dh, :, hi], at_x(3))
            rs_push(c, "b%d+" % dh, ps.at[c, dh * 4 + 2, near, c1a], r_b.at[c, dh, :, c1a], at_x(1))
            rs_push(c, "b%d-" % dh, ps.at[c, dh * 4 + 2, near, c1b], r_b.at[c, dh, :, c1b], at_x(3))

    def add(c, i, rows, cols, *terms):
        total = ps[c, i, rows, cols].astype(F32)
        for term in terms:
            total = total + term.astype(F32)
        return total.astype(BF16)

    def grow(c, i, rows, cols, *terms):
        ps[c, i, rows, cols] = add(c, i, rows, cols, *terms)

    def r1a(c):
        for dh in range(2):
            plus, minus = dh * 4 + 3, dh * 4 + 1
            rs_wait(c, "a%d+" % dh, "a%d-" % dh)
            grow(c, plus, away, lo, r_a[c, dh, :, lo])
            grow(c, minus, away, hi, r_a[c, dh, :, hi])
            rs_push(c, "m%d+" % dh, ps.at[c, plus, away], r_m.at[c, dh, 0], at_x(1))
            rs_push(c, "m%d-" % dh, ps.at[c, minus, away], r_m.at[c, dh, 1], at_x(3))

    def r1b(c):
        for dh in range(2):
            plus, minus = dh * 4 + 3, dh * 4 + 1
            rs_wait(c, "b%d+" % dh, "b%d-" % dh)
            grow(c, plus, near, c1a, r_b[c, dh, :, c1a])
            grow(c, minus, near, c1b, r_b[c, dh, :, c1b])
            rs_push(c, "n%d+" % dh, ps.at[c, plus, near, c1], r_m0.at[c, dh, 0], at_x(1))
            rs_push(c, "n%d-" % dh, ps.at[c, minus, near, c1], r_m0.at[c, dh, 1], at_x(3))

    def r1c(c):
        rs_wait(c, "y")
        grow(c, 2, near, c2, r_y[c, 2])
        rs_push(c, "h+", ps.at[c, 2, near, c2a], r_h2.at[c, :, 0:H2], at_x(1))
        rs_push(c, "h-", ps.at[c, 2, near, c2b], r_h2.at[c, :, H2:W2], at_x(3))

    def send_back(c, j, src, dst, at, send_sem, recv_sem, blk):
        k = c * SEND + j
        if k == OWN:
            dst[at, :] = src[at, :]
        else:
            message(src.at[at], dst.at[at], send_sem.at[c], recv_sem.at[c], at_ep(k, -1, blk))

    def to_messages(rows):
        tall = jnp.concatenate([rows[:, i * QW : (i + 1) * QW] for i in range(4)], axis=0)
        return jnp.dot(p_back[...], tall, preferred_element_type=F32).astype(BF16)

    def r2a(c):
        rs_wait(c, "h+", "h-")
        for i, a in ((3, 0), (1, 1)):
            for half, cols in enumerate((c2a, c2b)):
                part = slice(half * H2, (half + 1) * H2)
                terms = [r_y[c, i, :, part]]
                if half == a:
                    terms.append(r_h2[c, :, part])
                ps[c, i, near, cols] = add(c, i, near, cols, *terms)
        rs_push(c, "k+", ps.at[c, 3, near, c2], r_m2.at[c, 0], at_x(1))
        rs_push(c, "k-", ps.at[c, 1, near, c2], r_m2.at[c, 1], at_x(3))

    def r2b(c):
        rs_wait(c, "n1+", "n1-")
        ps[c, 4, near, c1] = add(c, 4, near, c1, r_m0[c, 1, 0], r_m0[c, 1, 1])
        rs_push(c, "t", ps.at[c, 4, near, c1], r_t.at[c], at_y)

    def r2c(c):
        rs_wait(c, "m0+", "m0-", "m1+", "m1-")
        fin[...] = add(c, 0, away, every, r_m[c, 0, 0], r_m[c, 0, 1])
        fin2[...] = add(c, 4, away, every, r_m[c, 1, 0], r_m[c, 1, 1])
        ret_out[c * M + MH : (c + 1) * M, :] = to_messages(fin)
        ret_out2[c * MH : (c + 1) * MH, :] = to_messages(fin2)
        for j in range(SEND // 2, SEND):
            k = c * SEND + j
            send_back(c, j, ret_out, ret_in, near_at(k), s_ret, r_ret, b)
            send_back(c, j, ret_out2, ret_in2, far_at(k), s_ret2, r_ret2, b_other)

    def r3(c):
        rs_wait(c, "n0+", "n0-", "t", "k+", "k-")
        fin[:, c1] = add(c, 0, near, c1, r_m0[c, 0, 0], r_m0[c, 0, 1], r_t[c])
        fin[:, c2] = add(c, 0, near, c2, r_y[c, 0], r_m2[c, 0], r_m2[c, 1])
        ret_out[c * M : c * M + MH, :] = to_messages(fin)
        for j in range(SEND // 2):
            send_back(c, j, ret_out, ret_in, near_at(c * SEND + j), s_ret, r_ret, b)

    def k1(c):
        forward_keys()

    def at(c):
        if c == 0:
            attend_start()
        attend(2 * c, 2)

    def r0_first(c):
        if c == 0:
            for cp in local[4:7]:
                cp.wait()
        r0(c)

    attn_out = pltpu.make_async_copy(attn_ref, attn_hbm, s_loc.at[8])
    pieces = dict(
        A0=a0, A1a=a1a, A1b=a1b, A1c=a1c, A2a=a2a, A2b=a2b, R0=r0_first,
        R1a=r1a, R1b=r1b, R1c=r1c, R2a=r2a, R2b=r2b, R2c=r2c, R3=r3, K0=k0, K1=k1, AT=at, M=m,
    )
    for name, c in ORDER:
        pieces[name](c)
    attn_out.start()

    def returned(first, last):
        for c in range(first, last):
            wait_messages(ret_in, r_ret, c)
            wait_part(ret_in2.at[c * MH : (c + 1) * MH], r_ret2.at[c])
        one, two = slice(first * M, last * M), slice(first * MH, last * MH)
        return jnp.dot(gath[:, one], ret_in[one, :], preferred_element_type=F32) + jnp.dot(
            gath2[:, two], ret_in2[two, :], preferred_element_type=F32
        )

    acc[...] = returned(0, NC - 1)
    for cp in sent:
        cp.wait_send()
    for c in range(NC):
        wait_messages(out_msg, s_a2a, c)
        wait_part(in_msg2.at[c * MH : (c + 1) * MH], s_a2a2.at[c])
    acc[...] += returned(NC - 1, NC)
    moe_out = []
    for quarter in range(4):
        cols = slice(quarter * QW, (quarter + 1) * QW)
        moe_ref[:, cols] = acc[quarter * TOK : (quarter + 1) * TOK, :].astype(BF16)
        moe_out.append(
            pltpu.make_async_copy(moe_ref.at[:, cols], moe_hbm.at[:, cols], s_loc.at[9 + quarter])
        )
        moe_out[-1].start()
    for c in range(NC):
        wait_messages(ret_out, s_ret, c)
        wait_part(ret_out2.at[c * MH : (c + 1) * MH], s_ret2.at[c])
    attn_out.wait()
    for cp in moe_out:
        cp.wait()


def on_device(queries, keys, values, doc_lengths, hidden, norm_gain, token_ids, expert_table, w_gate, w_up, w_down):
    vmem = pl.BlockSpec(memory_space=pltpu.VMEM)
    hbm = pl.BlockSpec(memory_space=pl.ANY)
    dma = pltpu.SemaphoreType.DMA
    attended, moe = pl.pallas_call(
        layer_kernel,
        out_shape=(
            jax.ShapeDtypeStruct((TOK, HQ * HD), BF16),
            jax.ShapeDtypeStruct((TOK, D), BF16),
        ),
        in_specs=[pl.BlockSpec(memory_space=pltpu.SMEM)] + [vmem] * 2 + [hbm] * 8,
        out_specs=(hbm, hbm),
        scratch_shapes=[
            pltpu.VMEM((VROWS, 128), jnp.int32),
            pltpu.VMEM((TOK, D), BF16),
            pltpu.VMEM((TOK, HQ * HD), BF16),
            pltpu.VMEM((TOK, HQ * HD), BF16),
            pltpu.VMEM((TOK, D), BF16),
            pltpu.VMEM((5, 2, TOK, HK * HD), BF16),
            pltpu.VMEM((TOK, WIN), F32),
            pltpu.VMEM((2 * FB, D), BF16),
            pltpu.VMEM((FB, D), BF16),
            pltpu.VMEM((16, D), F32),
            pltpu.VMEM((4 * TOK, QW), BF16),
            pltpu.VMEM((NEP * 16, 4 * TOK), BF16),
            pltpu.VMEM((NEP * 16, QW), BF16),
            pltpu.VMEM((NEP * 16, QW), BF16),
            pltpu.VMEM((NEP * 8, QW), BF16),
            pltpu.VMEM((NEP * 16, QW), BF16),
            pltpu.VMEM((NEP * 8, QW), BF16),
            pltpu.VMEM((NEP * 16, QW), BF16),
            pltpu.VMEM((NEP * 8, QW), BF16),
            pltpu.VMEM((4 * R, M), BF16),
            pltpu.VMEM((4 * RH, MH), BF16),
            pltpu.VMEM((MH, 4 * RH), BF16),
            pltpu.VMEM((4 * TOK, NEP * 16), BF16),
            pltpu.VMEM((4 * TOK, NEP * 8), BF16),
            pltpu.VMEM((4 * TOK, QW), F32),
            pltpu.VMEM((NC, 8, R, D), BF16),
            pltpu.VMEM((NC, 8, R, D), BF16),
            pltpu.VMEM((NC, 2, RH, D), BF16),
            pltpu.VMEM((NC, 2, RH, W1), BF16),
            pltpu.VMEM((NC, 4, RH, W2), BF16),
            pltpu.VMEM((NC, 2, 2, RH, D), BF16),
            pltpu.VMEM((NC, 2, 2, RH, W1), BF16),
            pltpu.VMEM((NC, RH, W2), BF16),
            pltpu.VMEM((NC, 2, RH, W2), BF16),
            pltpu.VMEM((NC, RH, W1), BF16),
            pltpu.VMEM((RH, D), BF16),
            pltpu.VMEM((RH, D), BF16),
            dma((13,)),
            dma((6,)),
            dma((6,)),
            dma((NC,)),
            dma((NC,)),
            dma((NC,)),
            dma((NC,)),
            dma((NC,)),
            dma((NC,)),
            dma((NC,)),
            dma((NC,)),
            dma((NC, 16)),
            dma((NC, 16)),
            dma((NC, 22)),
            dma((NC, 22)),
        ],
        compiler_params=pltpu.CompilerParams(
            collective_id=0, has_side_effects=True, vmem_limit_bytes=62 * 2**20
        ),
        name="layer",
    )(
        doc_lengths,
        token_ids.reshape(1, TOK),
        norm_gain.reshape(D // 128, 128),
        expert_table.reshape(VROWS, 128),
        hidden.reshape(TOK, D),
        queries.reshape(TOK, HQ * HD),
        keys.reshape(TOK, HK * HD),
        values.reshape(TOK, HK * HD),
        w_gate.reshape(FB, D),
        w_up.reshape(FB, D),
        w_down.reshape(FB, D),
    )
    return attended[:, None, :], moe[:, None, :]


def solution(mesh):
    return jax.shard_map(
        on_device,
        mesh=mesh,
        in_specs=(
            P("blk", "ep", None),
            P("blk", "ep", None),
            P("blk", "ep", None),
            P("ep", None),
            P("blk", "ep", None),
            P(),
            P("blk", "ep"),
            P(),
            P("ep", "blk", None),
            P("ep", "blk", None),
            P("ep", "blk", None),
        ),
        out_specs=(P("blk", "ep", None), P("blk", "ep", None)),
        check_vma=False,
    )
```

```python
import functools
import math

import jax
import jax.numpy as jnp
from jax import lax
from jax.experimental import pallas as pl
from jax.experimental.pallas import tpu as pltpu
from jax.sharding import PartitionSpec as P

HQ = 48
HK = 8
HD = 128
GROUPS = HQ // HK
D = 5120
FB = 192
TOK = 128
CAP = 4
NX, NH, NZ = 4, 2, 8
NEP = 32
VROWS = 1184
QW = D // 4

NC = 4
SEND = NEP // NC
R = SEND * CAP
RH = R // 2
M = SEND * 16
MH = M // 2
Z_ORDER = (1, 7, 3, 5, 6, 4, 0, 2)
PZ = NZ // NC
OWN = (Z_ORDER.index(0) // PZ) * SEND + (Z_ORDER.index(0) % PZ) * 2
HALF = 2432
W1 = 1536
W2 = D - W1
H1, H2 = W1 // 2, W2 // 2
KEYS_FIRST = True
MESSAGES_FIRST = 4
ORDER = (
    ("A0", 0), ("A1b", 0), ("K1", 0), ("A0", 1), ("A1a", 0), ("A1c", 0), ("A2b", 0), ("A0", 2),
    ("A1a", 1), ("A0", 3), ("A1c", 1), ("A2a", 0), ("AT", 0), ("A1b", 1), ("AT", 1), ("A1a", 2),
    ("A1c", 2), ("AT", 2), ("A2a", 1), ("AT", 3), ("A1b", 2), ("A1a", 3), ("A1b", 3), ("AT", 4),
    ("R0", 0), ("A2b", 1), ("A1c", 3), ("A2a", 2), ("AT", 5), ("A2b", 2), ("A2a", 3), ("A2b", 3),
    ("R1a", 0), ("R1b", 0), ("R0", 1), ("AT", 6), ("R1c", 0), ("AT", 7), ("R0", 2), ("R2b", 0),
    ("R2c", 0), ("R0", 3), ("R2a", 0), ("R1a", 1), ("R1b", 1), ("R1c", 1), ("R1a", 2), ("R1b", 2),
    ("R1a", 3), ("R1b", 3), ("R1c", 2), ("R3", 0), ("R2c", 1), ("R2b", 1), ("R2a", 1), ("R1c", 3),
    ("R2c", 2), ("R2b", 2), ("R2c", 3), ("R2b", 3), ("R2a", 2), ("R3", 1), ("R2a", 3), ("R3", 2),
    ("R3", 3),
)
WIN = 5 * TOK
BLOCK_BACK = (0, 2, 4, 1, 3)

F32 = jnp.float32
BF16 = jnp.bfloat16
MESH = pl.DeviceIdType.MESH


def route(k):
    j = k % SEND
    return Z_ORDER[(k // SEND) * PZ + (j // 2) % PZ], j // (SEND // 2), j % 2


def iota(shape, dim):
    return lax.broadcasted_iota(jnp.int32, shape, dim)


def layer_kernel(
    doc_ref, tok_ref, gain_ref, table_hbm, hid_hbm, q_hbm, k_hbm, v_hbm, wg_hbm, wu_hbm, wd_hbm,
    attn_hbm, moe_hbm,
    table_ref, hid_ref, q_ref, attn_ref, moe_ref,
    kv, bias, wgu, wd, gain, normed, spread, out_msg, in_msg, in_msg2, ret_out, ret_out2, ret_in, ret_in2,
    p_near, p_far, p_back, gath, gath2, acc, xs, ps, r_a, r_b, r_y, r_m, r_m0, r_h2, r_m2, r_t, fin, fin2,
    s_loc, s_kv, r_kv, s_a2a, r_a2a, s_a2a2, r_a2a2, s_ret, r_ret, s_ret2, r_ret2, s_ag, r_ag, s_rs, r_rs,
):
    b = lax.axis_index("blk")
    e = lax.axis_index("ep")
    x, h = b // 2, b % 2
    z, yl, core = e // 4, (e // 2) % 2, e % 2
    b_other = x * 2 + (h + 1) % 2

    def at_x(step):
        return (((x + step) % NX) * 2 + h, e)

    at_y = (b_other, e)

    def at_ep(k, sign, blk):
        dz, fy, dc = route(k)
        zz = (z + (dz if sign > 0 else NZ - dz)) % NZ
        return (blk, (zz * 2 + (yl + fy) % 2) * 2 + (core + dc) % 2)

    barrier = pltpu.get_barrier_semaphore()
    far = [k for k in range(NEP) if route(k)[1] == 1]
    peers = [at_x(1), at_x(2), at_x(3), at_y]
    peers += [at_ep(k, 1, b) for k in range(NEP) if k != OWN]
    peers += [at_ep(k, 1, b_other) for k in far]
    for peer in peers:
        pl.semaphore_signal(barrier, inc=1, device_id=peer, device_id_type=MESH)

    local = []
    for i, (src, dst) in enumerate(
        (
            (hid_hbm, hid_ref),
            (table_hbm, table_ref),
            (k_hbm, kv.at[0, 0]),
            (v_hbm, kv.at[0, 1]),
            (wg_hbm, wgu.at[0:FB]),
            (wu_hbm, wgu.at[FB : 2 * FB]),
            (wd_hbm, wd),
            (q_hbm, q_ref),
        )
    ):
        cp = pltpu.make_async_copy(src, dst, s_loc.at[i])
        cp.start()
        local.append(cp)

    for j in range(D // 128):
        gain[:, j * 128 : (j + 1) * 128] = jnp.broadcast_to(gain_ref[j : j + 1, :].astype(F32), (16, 128))

    sent = []

    def push(src, dst, send_sem, recv_sem, device):
        cp = pltpu.make_async_remote_copy(
            src_ref=src, dst_ref=dst, send_sem=send_sem, recv_sem=recv_sem,
            device_id=device, device_id_type=MESH,
        )
        cp.start()
        sent.append(cp)
        return cp

    local[0].wait()

    def norm_rows(i, carry):
        rows = pl.ds(pl.multiple_of(i * 16, 16), 16)
        wide = hid_ref[rows, :].astype(F32)
        scale = lax.rsqrt(jnp.sum(wide * wide, axis=1, keepdims=True) * (1.0 / D) + 1e-05)
        out = (wide * scale * gain[...]).astype(BF16)
        for quarter in range(4):
            at = pl.ds(pl.multiple_of(quarter * TOK + i * 16, 16), 16)
            normed[at, :] = out[:, quarter * QW : (quarter + 1) * QW]
        return carry

    lax.fori_loop(0, TOK // 16, norm_rows, 0)

    pl.semaphore_wait(barrier, len(peers))

    kv_in = []

    def k0(c):
        for i, src in ((0, k_hbm), (1, v_hbm)):
            kv_in.append(
                push(src, kv.at[c + 1, i], s_kv.at[2 * c + i], r_kv.at[2 * c + i], at_x(c + 1))
            )

    if KEYS_FIRST:
        k0(0)
        k0(1)

    local[1].wait()
    eye = iota((TOK, TOK), 0) == iota((TOK, TOK), 1)
    lane = iota((TOK, TOK), 1)
    tok = tok_ref[...]
    tok_hi, tok_lo = (tok // 128).astype(F32), (tok % 128).astype(F32)
    hi_col = jnp.sum(jnp.where(eye, tok_hi, 0.0), axis=1, keepdims=True)
    lo_col = jnp.sum(jnp.where(eye, tok_lo, 0.0), axis=1, keepdims=True)
    pick = (iota((TOK, VROWS), 1).astype(F32) == hi_col).astype(F32).astype(BF16)
    row = jnp.dot(pick, table_ref[...].astype(F32).astype(BF16), preferred_element_type=F32)
    expert = jnp.sum(jnp.where(lane.astype(F32) == lo_col, row, 0.0), axis=1, keepdims=True)
    onehot = (lane.astype(F32) == expert).astype(F32)
    earlier = (lane < iota((TOK, TOK), 0)).astype(F32).astype(BF16)
    before = jnp.dot(earlier, onehot.astype(BF16), preferred_element_type=F32)
    rank = jnp.sum(before * onehot, axis=1, keepdims=True)
    slot_col = jnp.where(rank < CAP, expert * CAP + rank, -1.0)
    slot_row = jnp.sum(jnp.where(eye, slot_col, 0.0), axis=0, keepdims=True)

    def slot_of(k, i):
        j = k % SEND
        pos = (k // SEND) * PZ + (j // 2) % PZ
        dz = jnp.zeros_like(k)
        for p in range(NZ):
            dz = jnp.where(pos == p, Z_ORDER[p], dz)
        other = (((z + dz) % NZ) * 2 + (yl + j // (SEND // 2)) % 2) * 2 + (core + j % 2) % 2
        return (other * CAP + i % 4).astype(F32), (i // 4) % 4

    msg = iota((NEP * 16, TOK), 0)
    msg_slot, msg_quarter = slot_of(msg // 16, msg)
    here = msg_slot == slot_row
    for quarter in range(4):
        spread[:, quarter * TOK : (quarter + 1) * TOK] = (
            (here & (msg_quarter == quarter)).astype(F32).astype(BF16)
        )

    def spread_columns(n, carry):
        cols = pl.ds(pl.multiple_of(n * 256, 128), 256)
        out_msg[:, cols] = jnp.dot(
            spread[...], normed[:, cols], preferred_element_type=F32
        ).astype(BF16)
        return carry

    lax.fori_loop(0, QW // 256, spread_columns, 0)

    def message(src, dst, send_sem, recv_sem, device):
        pltpu.make_async_remote_copy(
            src_ref=src, dst_ref=dst, send_sem=send_sem, recv_sem=recv_sem,
            device_id=device, device_id_type=MESH,
        ).start()

    def far_at(k):
        start = (k // SEND) * MH + (k % SEND - SEND // 2) * 16
        return slice(start, start + 16)

    def near_at(k):
        return slice(k * 16, (k + 1) * 16)

    def m(c):
        for k in range(c * SEND, (c + 1) * SEND):
            at = near_at(k)
            if k == OWN:
                in_msg[at, :] = out_msg[at, :]
            else:
                message(out_msg.at[at], in_msg.at[at], s_a2a.at[c], r_a2a.at[c], at_ep(k, 1, b))
            if k in far:
                message(
                    out_msg.at[at], in_msg2.at[far_at(k)], s_a2a2.at[c], r_a2a2.at[c],
                    at_ep(k, 1, b_other),
                )

    for c in range(MESSAGES_FIRST):
        m(c)

    def wait_part(part, sem):
        pltpu.make_async_copy(part, part, sem).wait()

    def wait_messages(ref, sem, c):
        if c == OWN // SEND:
            first = OWN * 16
            wait_part(ref.at[first + 16 : (c + 1) * M], sem.at[c])
        else:
            wait_part(ref.at[c * M : (c + 1) * M], sem.at[c])

    last = 0
    ends = []
    for i in range(8):
        last = last + doc_ref[0, i]
        ends.append(last)
    q_pos = b * TOK + iota((TOK, TOK), 0)
    start = jnp.zeros((TOK, TOK), jnp.int32)
    for end in ends:
        start = jnp.where(q_pos >= end, end, start)
    for s, back in enumerate(BLOCK_BACK):
        k_pos = (b - back) * TOK + iota((TOK, TOK), 1)
        allowed = (k_pos >= start) & (k_pos <= q_pos)
        bias[:, s * TOK : (s + 1) * TOK] = jnp.where(allowed, 0.0, -1e30).astype(F32)

    kv_fwd = []

    def forward_keys():
        for cp in kv_in:
            cp.wait_recv()
        local[2].wait()
        local[3].wait()
        for i in range(2):
            kv_fwd.append(push(kv.at[h + i], kv.at[3 + i], s_kv.at[4 + i], r_kv.at[4 + i], at_y))

    def attend_start():
        for cp in kv_fwd:
            cp.wait_recv()
        local[7].wait()

    def attend(first, count):
        def one(g, carry):
            head = pl.ds(pl.multiple_of(g * HD, HD), HD)
            wide = pl.ds(pl.multiple_of(g * GROUPS * HD, HD), GROUPS * HD)
            keys = kv[:, 0, :, head].reshape(WIN, HD)
            vals = kv[:, 1, :, head].reshape(WIN, HD)
            q_all = q_ref[:, wide]
            outs = []
            for i in range(GROUPS):
                q_one = q_all[:, i * HD : (i + 1) * HD]
                score = lax.dot_general(
                    q_one, keys, (((1,), (1,)), ((), ())), preferred_element_type=F32
                ) + bias[...]
                top = jnp.max(score, axis=1, keepdims=True)
                weight = jnp.exp((score - top) * (1.0 / math.sqrt(HD)))
                total = jnp.sum(weight, axis=1, keepdims=True)
                mixed = jnp.dot(weight.astype(BF16), vals, preferred_element_type=F32)
                outs.append((mixed / total).astype(BF16))
            attn_ref[:, wide] = jnp.concatenate(outs, axis=1)
            return carry

        lax.fori_loop(first, first + count, one, 0)

    def perm(count, row_dim):
        rr, mm = iota((4 * count, 4 * count), row_dim), iota((4 * count, 4 * count), 1 - row_dim)
        row = rr % count
        same = (mm // 16 == row // 4) & ((mm // 4) % 4 == rr // count) & (mm % 4 == row % 4)
        return same.astype(F32).astype(BF16)

    p_near[...] = perm(R, 0)
    p_far[...] = perm(RH, 0)
    p_back[...] = perm(RH, 1)

    def collect(ref, k, i):
        col_slot, col_quarter = slot_of(k, i)
        mine = col_slot == slot_col
        for quarter in range(4):
            ref[quarter * TOK : (quarter + 1) * TOK, :] = (
                (mine & (col_quarter == quarter)).astype(F32).astype(BF16)
            )

    i1, i2 = iota((TOK, NEP * 16), 1), iota((TOK, NEP * 8), 1)
    collect(gath, i1 // 16, i1)
    collect(gath2, (i2 // MH) * SEND + SEND // 2 + (i2 % MH) // 16, i2)

    ag = [dict() for _ in range(NC)]
    rs = [dict() for _ in range(NC)]

    def ag_push(c, name, src, dst, device):
        i = len(ag[c])
        ag[c][name] = push(src, dst, s_ag.at[c, i], r_ag.at[c, i], device)

    def rs_push(c, name, src, dst, device):
        i = len(rs[c])
        rs[c][name] = push(src, dst, s_rs.at[c, i], r_rs.at[c, i], device)

    def ag_wait(c, *names):
        for name in names:
            ag[c][name].wait_recv()

    def rs_wait(c, *names):
        for name in names:
            rs[c][name].wait_recv()

    every, lo, hi = slice(0, D), slice(0, HALF), slice(HALF, D)
    c1, c2 = slice(0, W1), slice(W1, D)
    c1a, c1b = slice(0, H1), slice(H1, W1)
    c2a, c2b = slice(W1, W1 + H2), slice(W1 + H2, D)
    allr, near, away = slice(0, R), slice(0, RH), slice(RH, R)

    def a0(c):
        wait_messages(in_msg, r_a2a, c)
        wait_part(in_msg2.at[c * MH : (c + 1) * MH], r_a2a2.at[c])
        own = jnp.dot(p_near[...], in_msg[c * M : (c + 1) * M, :], preferred_element_type=F32).astype(BF16)
        two = jnp.dot(p_far[...], in_msg2[c * MH : (c + 1) * MH, :], preferred_element_type=F32).astype(BF16)
        for quarter in range(4):
            cols = slice(quarter * QW, (quarter + 1) * QW)
            xs[c, 0, :, cols] = own[quarter * R : (quarter + 1) * R, :]
            xs[c, 4, away, cols] = two[quarter * RH : (quarter + 1) * RH, :]
        ag_push(c, "1", xs.at[c, 0], xs.at[c, 1], at_x(1))
        ag_push(c, "3", xs.at[c, 0], xs.at[c, 3], at_x(3))
        ag_push(c, "4", xs.at[c, 0, near], xs.at[c, 4, near], at_y)
        ag_push(c, "5f", xs.at[c, 4, away], xs.at[c, 5, away], at_x(1))
        ag_push(c, "7f", xs.at[c, 4, away], xs.at[c, 7, away], at_x(3))

    def hop(c, name, i, j, rows, cols, device):
        ag_push(c, name, xs.at[c, i, rows, cols], xs.at[c, j, rows, cols], device)

    def a1a(c):
        ag_wait(c, "1", "3")
        hop(c, "2a", 1, 2, allr, lo, at_x(1))
        hop(c, "2b", 3, 2, allr, hi, at_x(3))
        hop(c, "5y", 1, 5, near, c2, at_y)
        hop(c, "7y", 3, 7, near, c2, at_y)

    def a1b(c):
        ag_wait(c, "4")
        hop(c, "5x", 4, 5, near, c1, at_x(1))
        hop(c, "7x", 4, 7, near, c1, at_x(3))

    def a1c(c):
        ag_wait(c, "5f", "7f")
        hop(c, "6fa", 5, 6, away, lo, at_x(1))
        hop(c, "6fb", 7, 6, away, hi, at_x(3))

    def a2a(c):
        ag_wait(c, "2a", "2b")
        hop(c, "6y", 2, 6, near, c2, at_y)

    def a2b(c):
        ag_wait(c, "5x", "7x")
        hop(c, "6a", 5, 6, near, c1a, at_x(1))
        hop(c, "6b", 7, 6, near, c1b, at_x(3))

    def r0(c):
        ag_wait(c, "5y", "7y", "6fa", "6fb", "6a", "6b", "6y")
        rows = xs[c].reshape(8 * R, D)
        both = lax.dot_general(
            rows, wgu[...], (((1,), (1,)), ((), ())), preferred_element_type=F32
        )
        gate, up = both[:, :FB], both[:, FB:]
        act = (gate / (1.0 + jnp.exp(-gate)) * up).astype(BF16)

        def down(n, carry):
            cols = pl.ds(pl.multiple_of(n * 512, 128), 512)
            res = jnp.dot(act, wd[:, cols], preferred_element_type=F32).astype(BF16)
            ps[c, :, :, cols] = res.reshape(8, R, 512)
            return carry

        lax.fori_loop(0, D // 512, down, 0)
        rs_push(c, "y", ps.at[c, 4:8, near, c2], r_y.at[c], at_y)
        for dh in range(2):
            rs_push(c, "a%d+" % dh, ps.at[c, dh * 4 + 2, away, lo], r_a.at[c, dh, :, lo], at_x(1))
            rs_push(c, "a%d-" % dh, ps.at[c, dh * 4 + 2, away, hi], r_a.at[c, dh, :, hi], at_x(3))
            rs_push(c, "b%d+" % dh, ps.at[c, dh * 4 + 2, near, c1a], r_b.at[c, dh, :, c1a], at_x(1))
            rs_push(c, "b%d-" % dh, ps.at[c, dh * 4 + 2, near, c1b], r_b.at[c, dh, :, c1b], at_x(3))

    def add(c, i, rows, cols, *terms):
        total = ps[c, i, rows, cols].astype(F32)
        for term in terms:
            total = total + term.astype(F32)
        return total.astype(BF16)

    def grow(c, i, rows, cols, *terms):
        ps[c, i, rows, cols] = add(c, i, rows, cols, *terms)

    def r1a(c):
        for dh in range(2):
            plus, minus = dh * 4 + 3, dh * 4 + 1
            rs_wait(c, "a%d+" % dh, "a%d-" % dh)
            grow(c, plus, away, lo, r_a[c, dh, :, lo])
            grow(c, minus, away, hi, r_a[c, dh, :, hi])
            rs_push(c, "m%d+" % dh, ps.at[c, plus, away], r_m.at[c, dh, 0], at_x(1))
            rs_push(c, "m%d-" % dh, ps.at[c, minus, away], r_m.at[c, dh, 1], at_x(3))

    def r1b(c):
        for dh in range(2):
            plus, minus = dh * 4 + 3, dh * 4 + 1
            rs_wait(c, "b%d+" % dh, "b%d-" % dh)
            grow(c, plus, near, c1a, r_b[c, dh, :, c1a])
            grow(c, minus, near, c1b, r_b[c, dh, :, c1b])
            rs_push(c, "n%d+" % dh, ps.at[c, plus, near, c1], r_m0.at[c, dh, 0], at_x(1))
            rs_push(c, "n%d-" % dh, ps.at[c, minus, near, c1], r_m0.at[c, dh, 1], at_x(3))

    def r1c(c):
        rs_wait(c, "y")
        grow(c, 2, near, c2, r_y[c, 2])
        rs_push(c, "h+", ps.at[c, 2, near, c2a], r_h2.at[c, :, 0:H2], at_x(1))
        rs_push(c, "h-", ps.at[c, 2, near, c2b], r_h2.at[c, :, H2:W2], at_x(3))

    def send_back(c, j, src, dst, at, send_sem, recv_sem, blk):
        k = c * SEND + j
        if k == OWN:
            dst[at, :] = src[at, :]
        else:
            message(src.at[at], dst.at[at], send_sem.at[c], recv_sem.at[c], at_ep(k, -1, blk))

    def to_messages(rows):
        tall = jnp.concatenate([rows[:, i * QW : (i + 1) * QW] for i in range(4)], axis=0)
        return jnp.dot(p_back[...], tall, preferred_element_type=F32).astype(BF16)

    def r2a(c):
        rs_wait(c, "h+", "h-")
        for i, a in ((3, 0), (1, 1)):
            for half, cols in enumerate((c2a, c2b)):
                part = slice(half * H2, (half + 1) * H2)
                terms = [r_y[c, i, :, part]]
                if half == a:
                    terms.append(r_h2[c, :, part])
                ps[c, i, near, cols] = add(c, i, near, cols, *terms)
        rs_push(c, "k+", ps.at[c, 3, near, c2], r_m2.at[c, 0], at_x(1))
        rs_push(c, "k-", ps.at[c, 1, near, c2], r_m2.at[c, 1], at_x(3))

    def r2b(c):
        rs_wait(c, "n1+", "n1-")
        ps[c, 4, near, c1] = add(c, 4, near, c1, r_m0[c, 1, 0], r_m0[c, 1, 1])
        rs_push(c, "t", ps.at[c, 4, near, c1], r_t.at[c], at_y)

    def r2c(c):
        rs_wait(c, "m0+", "m0-", "m1+", "m1-")
        fin[...] = add(c, 0, away, every, r_m[c, 0, 0], r_m[c, 0, 1])
        fin2[...] = add(c, 4, away, every, r_m[c, 1, 0], r_m[c, 1, 1])
        ret_out[c * M + MH : (c + 1) * M, :] = to_messages(fin)
        ret_out2[c * MH : (c + 1) * MH, :] = to_messages(fin2)
        for j in range(SEND // 2, SEND):
            k = c * SEND + j
            send_back(c, j, ret_out, ret_in, near_at(k), s_ret, r_ret, b)
            send_back(c, j, ret_out2, ret_in2, far_at(k), s_ret2, r_ret2, b_other)

    def r3(c):
        rs_wait(c, "n0+", "n0-", "t", "k+", "k-")
        fin[:, c1] = add(c, 0, near, c1, r_m0[c, 0, 0], r_m0[c, 0, 1], r_t[c])
        fin[:, c2] = add(c, 0, near, c2, r_y[c, 0], r_m2[c, 0], r_m2[c, 1])
        ret_out[c * M : c * M + MH, :] = to_messages(fin)
        for j in range(SEND // 2):
            send_back(c, j, ret_out, ret_in, near_at(c * SEND + j), s_ret, r_ret, b)

    def k1(c):
        forward_keys()

    def at(c):
        if c == 0:
            attend_start()
        attend(c, 1)

    def r0_first(c):
        if c == 0:
            for cp in local[4:7]:
                cp.wait()
        r0(c)

    attn_out = pltpu.make_async_copy(attn_ref, attn_hbm, s_loc.at[8])
    pieces = dict(
        A0=a0, A1a=a1a, A1b=a1b, A1c=a1c, A2a=a2a, A2b=a2b, R0=r0_first,
        R1a=r1a, R1b=r1b, R1c=r1c, R2a=r2a, R2b=r2b, R2c=r2c, R3=r3, K0=k0, K1=k1, AT=at, M=m,
    )
    for name, c in ORDER:
        pieces[name](c)
    attn_out.start()

    def returned(first, last):
        for c in range(first, last):
            wait_messages(ret_in, r_ret, c)
            wait_part(ret_in2.at[c * MH : (c + 1) * MH], r_ret2.at[c])
        one, two = slice(first * M, last * M), slice(first * MH, last * MH)
        return jnp.dot(gath[:, one], ret_in[one, :], preferred_element_type=F32) + jnp.dot(
            gath2[:, two], ret_in2[two, :], preferred_element_type=F32
        )

    acc[...] = returned(0, NC - 1)
    for cp in sent:
        cp.wait_send()
    for c in range(NC):
        wait_messages(out_msg, s_a2a, c)
        wait_part(in_msg2.at[c * MH : (c + 1) * MH], s_a2a2.at[c])
    acc[...] += returned(NC - 1, NC)
    moe_out = []
    for quarter in range(4):
        cols = slice(quarter * QW, (quarter + 1) * QW)
        moe_ref[:, cols] = acc[quarter * TOK : (quarter + 1) * TOK, :].astype(BF16)
        moe_out.append(
            pltpu.make_async_copy(moe_ref.at[:, cols], moe_hbm.at[:, cols], s_loc.at[9 + quarter])
        )
        moe_out[-1].start()
    for c in range(NC):
        wait_messages(ret_out, s_ret, c)
        wait_part(ret_out2.at[c * MH : (c + 1) * MH], s_ret2.at[c])
    attn_out.wait()
    for cp in moe_out:
        cp.wait()


def on_device(queries, keys, values, doc_lengths, hidden, norm_gain, token_ids, expert_table, w_gate, w_up, w_down):
    vmem = pl.BlockSpec(memory_space=pltpu.VMEM)
    hbm = pl.BlockSpec(memory_space=pl.ANY)
    dma = pltpu.SemaphoreType.DMA
    attended, moe = pl.pallas_call(
        layer_kernel,
        out_shape=(
            jax.ShapeDtypeStruct((TOK, HQ * HD), BF16),
            jax.ShapeDtypeStruct((TOK, D), BF16),
        ),
        in_specs=[pl.BlockSpec(memory_space=pltpu.SMEM)] + [vmem] * 2 + [hbm] * 8,
        out_specs=(hbm, hbm),
        scratch_shapes=[
            pltpu.VMEM((VROWS, 128), jnp.int32),
            pltpu.VMEM((TOK, D), BF16),
            pltpu.VMEM((TOK, HQ * HD), BF16),
            pltpu.VMEM((TOK, HQ * HD), BF16),
            pltpu.VMEM((TOK, D), BF16),
            pltpu.VMEM((5, 2, TOK, HK * HD), BF16),
            pltpu.VMEM((TOK, WIN), F32),
            pltpu.VMEM((2 * FB, D), BF16),
            pltpu.VMEM((FB, D), BF16),
            pltpu.VMEM((16, D), F32),
            pltpu.VMEM((4 * TOK, QW), BF16),
            pltpu.VMEM((NEP * 16, 4 * TOK), BF16),
            pltpu.VMEM((NEP * 16, QW), BF16),
            pltpu.VMEM((NEP * 16, QW), BF16),
            pltpu.VMEM((NEP * 8, QW), BF16),
            pltpu.VMEM((NEP * 16, QW), BF16),
            pltpu.VMEM((NEP * 8, QW), BF16),
            pltpu.VMEM((NEP * 16, QW), BF16),
            pltpu.VMEM((NEP * 8, QW), BF16),
            pltpu.VMEM((4 * R, M), BF16),
            pltpu.VMEM((4 * RH, MH), BF16),
            pltpu.VMEM((MH, 4 * RH), BF16),
            pltpu.VMEM((4 * TOK, NEP * 16), BF16),
            pltpu.VMEM((4 * TOK, NEP * 8), BF16),
            pltpu.VMEM((4 * TOK, QW), F32),
            pltpu.VMEM((NC, 8, R, D), BF16),
            pltpu.VMEM((NC, 8, R, D), BF16),
            pltpu.VMEM((NC, 2, RH, D), BF16),
            pltpu.VMEM((NC, 2, RH, W1), BF16),
            pltpu.VMEM((NC, 4, RH, W2), BF16),
            pltpu.VMEM((NC, 2, 2, RH, D), BF16),
            pltpu.VMEM((NC, 2, 2, RH, W1), BF16),
            pltpu.VMEM((NC, RH, W2), BF16),
            pltpu.VMEM((NC, 2, RH, W2), BF16),
            pltpu.VMEM((NC, RH, W1), BF16),
            pltpu.VMEM((RH, D), BF16),
            pltpu.VMEM((RH, D), BF16),
            dma((13,)),
            dma((6,)),
            dma((6,)),
            dma((NC,)),
            dma((NC,)),
            dma((NC,)),
            dma((NC,)),
            dma((NC,)),
            dma((NC,)),
            dma((NC,)),
            dma((NC,)),
            dma((NC, 16)),
            dma((NC, 16)),
            dma((NC, 22)),
            dma((NC, 22)),
        ],
        compiler_params=pltpu.CompilerParams(
            collective_id=0, has_side_effects=True, vmem_limit_bytes=62 * 2**20
        ),
        name="layer",
    )(
        doc_lengths,
        token_ids.reshape(1, TOK),
        norm_gain.reshape(D // 128, 128),
        expert_table.reshape(VROWS, 128),
        hidden.reshape(TOK, D),
        queries.reshape(TOK, HQ * HD),
        keys.reshape(TOK, HK * HD),
        values.reshape(TOK, HK * HD),
        w_gate.reshape(FB, D),
        w_up.reshape(FB, D),
        w_down.reshape(FB, D),
    )
    return attended[:, None, :], moe[:, None, :]


def solution(mesh):
    return jax.shard_map(
        on_device,
        mesh=mesh,
        in_specs=(
            P("blk", "ep", None),
            P("blk", "ep", None),
            P("blk", "ep", None),
            P("ep", None),
            P("blk", "ep", None),
            P(),
            P("blk", "ep"),
            P(),
            P("ep", "blk", None),
            P("ep", "blk", None),
            P("ep", "blk", None),
        ),
        out_specs=(P("blk", "ep", None), P("blk", "ep", None)),
        check_vma=False,
    )
```
